32 devices in a mesh: groups: 2 (over y), dp: 8 (over z, x), fsdp: 2 (over core).
Axes of the slice: x: 2, y: 2, z: 4, core: 2. Of those that a mesh axis runs over, the one named last changes fastest.
Arguments:
- layer_input: bfloat16 [4096, 8192], P(('groups', 'dp'), 'fsdp'), parts along dimension 0, may hold values from -6 to 6
- w_value: bfloat16 [8192, 128], P('fsdp', 'dp'), may hold values from -0.0625 to 0.0625
- queries: bfloat16 [4096, 1024], P(('groups', 'dp'), 'fsdp'), parts along dimension 0, may hold values from -16 to 16
- keys: bfloat16 [4096, 128], P(('groups', 'dp')), parts along dimension 0, may hold values from -16 to 16
- grad_out: bfloat16 [4096, 1024], P(('groups', 'dp'), 'fsdp'), parts along dimension 0, may hold values from -6 to 6
- doc_lengths: int32 [8], P('groups'), parts along dimension 0, may hold values from 1 to 768, 2048 in all
- prefix_spans: int32 [8], P('groups'), parts along dimension 0, may hold values from 1 to 768
Outputs:
- grad_input: bfloat16 [4096, 8192], P(('groups', 'dp'), 'fsdp'), parts along dimension 0
- grad_queries: bfloat16 [4096, 1024], P(('groups', 'dp'), 'fsdp'), parts along dimension 0
- grad_keys: bfloat16 [4096, 128], P(('groups', 'dp')), parts along dimension 0
- grad_weight: float32 [16384, 128], P(('groups', 'fsdp'), 'dp'), parts along dimension 0
The draws below stay inside these ranges and needn't reach their ends.
There are 2 independent parts, one for each index of `groups`. The reference program is written for one: setup_inputs(seed, part) draws one part's arguments, and reference() takes and returns one part's arrays. A program takes and returns all parts, laid end to end along the dimension named above; an argument that names none is the same for every part. Nothing has to cross between parts.
Inputs may be any that keep to these rules, and one draw needn't show every extreme that they name: `doc_lengths`: the lengths sum to 2048 and one of them equals 768.
All inputs are finite; a program needn't handle non-finite values.
Results may differ from the reference program's by a relative error of at most 0.0065.
Values may be sent and summed in bfloat16 or wider, within the bound.
No kernel may reach another device: no remote copies, remote signals or barrier semaphores. Data moves between devices by JAX's collectives and lax.ppermute only.
A program may use at most 128 MiB of HBM per device.

```python
import math
import jax
import jax.numpy as jnp
import numpy as np
from jax import lax

D = 8192
HD = 128
GROUP = 8
TOK_DEV = 256
SPAN = 3
TOKENS = 2048
DOC_MAX = 768
NDOCS = 4
N_DP = 8


def draw_keys(key, part):
    key = jax.random.fold_in(key, 1)
    values = jnp.clip(jax.random.normal(key, (TOKENS, HD), jnp.float32), -6.0, 6.0)
    return values.astype(jnp.bfloat16)


def draw_queries(key, part):
    key = jax.random.fold_in(key, 2)
    values = jnp.clip(jax.random.normal(key, (TOKENS, GROUP * HD), jnp.float32), -6.0, 6.0)
    return values.astype(jnp.bfloat16)


def plant(entries, key, smallest, top_value):
    longest = entries.shape.index(max(entries.shape))
    spots = []
    for shift in (0, 1):
        where = [jax.random.randint(jax.random.fold_in(key, axis), (), 0, length) for axis, length in enumerate(entries.shape)]
        where[longest] = (where[longest] + shift) % entries.shape[longest]
        spots.append(tuple(where))
    return entries.at[spots[0]].set(smallest).at[spots[1]].set(top_value)


def block_scale(rng, extent, cuts, low, largest):
    def one(axis_at, parts):
        heights = jax.random.uniform(jax.random.fold_in(jax.random.fold_in(rng, 6), axis_at), (parts,), jnp.float32, low / len(cuts), largest / len(cuts))
        return jnp.repeat(jnp.exp(heights), extent[axis_at] // parts).reshape((-1,) + (1,) * (len(extent) - axis_at - 1))

    level = one(*cuts[0])
    for cut in cuts[1:]:
        level = level * one(*cut)
    return level


def profile(count, total, most, skew):
    portions = [(1 << 20) // math.isqrt(grade ** skew) + 1 for grade in range(2, count + 1)]
    rest, holding = total - most - (count - 1), [1] * (count - 1)
    while rest > 0:
        free = [i for i in range(count - 1) if holding[i] < most]
        mass, budget = sum([portions[i] for i in free]), rest
        for i in free:
            extra = min(most - holding[i], max(1, budget * portions[i] // mass), rest)
            holding[i] = holding[i] + extra
            rest = rest - extra
    return np.array([most] + holding)


def ragged_sizes(rng, count, total, most, slope):
    if count == 2:
        one = jax.random.randint(rng, (), max(1, total - most), min(most, total - 1) + 1)
        return jnp.stack([one, total - one])
    lengths = jnp.asarray(profile(count, total, most, slope), jnp.int32)
    pairs = (count - 1) // 2
    giver, sink = lengths[1:1 + 2 * pairs:2], lengths[2:2 + 2 * pairs:2]
    margin = jnp.minimum(giver - 1, most - sink)
    passed = jax.random.randint(jax.random.fold_in(rng, 1), (pairs,), 0, 1 << 20) % (margin + 1)
    lengths = lengths.at[1:1 + 2 * pairs:2].set(giver - passed).at[2:2 + 2 * pairs:2].set(sink + passed)
    return lengths[jax.random.permutation(jax.random.fold_in(rng, 2), count)]


def centred(own_key, extent, deviation, most, pieces=(), kind=jnp.bfloat16):
    gain = block_scale(own_key, extent, pieces, -0.22, 0.18) if pieces else 1.0
    array = jax.random.normal(own_key, extent, jnp.float32) * deviation * gain
    return jnp.minimum(jnp.maximum(array, -most), most).astype(kind)


def setup_inputs(seed: int = 0, part: int = 0) -> dict:
    streams_of = jax.random.split(jax.random.key(seed), 8)
    part_keys = jax.random.split(jax.random.fold_in(streams_of[7], part), 8)
    return {
        "layer_input": centred(part_keys[0], (TOKENS, D), 1.0, 6.0, ((0, 8), (1, 2))),
        "w_value": centred(streams_of[1], (D, HD), D ** -0.5, 0.0625, ((0, 2), (1, 8))),
        "queries": draw_queries(jax.random.fold_in(jax.random.fold_in(streams_of[7], part), 71), part),
        "keys": draw_keys(jax.random.fold_in(jax.random.fold_in(streams_of[7], part), 71), part),
        "grad_out": centred(part_keys[4], (TOKENS, GROUP * HD), 1.0, 6.0, ((0, 8), (1, 2))),
        "doc_lengths": ragged_sizes(part_keys[5], NDOCS, TOKENS, DOC_MAX, 2).astype(jnp.int32),
        "prefix_spans": plant(jax.random.randint(part_keys[6], (NDOCS,), 1, DOC_MAX + 1), jax.random.fold_in(part_keys[6], 1), 1, DOC_MAX).astype(jnp.int32),
    }


NEGATIVE = -1e+30

def doc_tables(doc_lengths, prefix_spans):
    ends = jnp.cumsum(doc_lengths).astype(jnp.int32)
    starts = (ends - doc_lengths).astype(jnp.int32)
    prefix_end = (starts + jnp.minimum(prefix_spans, doc_lengths)).astype(jnp.int32)
    return (ends, prefix_end)

def locate(positions, ends, prefix_end):
    document = lax.optimization_barrier(jnp.sum((positions[:, None] >= ends[None, :]).astype(jnp.int32), axis=1)).astype(jnp.int32)
    members = document[:, None] == jnp.arange(ends.shape[0], dtype=jnp.int32)[None, :]
    bound = lax.optimization_barrier(jnp.sum(jnp.where(members, prefix_end[None, :], 0), axis=1)).astype(jnp.int32)
    return (document, bound)

def visible_mask(query_positions, key_positions, ends, prefix_end, total_rows):
    query_doc, query_bound = locate(query_positions, ends, prefix_end)
    key_doc, unused_bound = locate(key_positions, ends, prefix_end)
    inside = (key_positions >= 0) & (key_positions < total_rows)
    same_doc = query_doc[:, None] == key_doc[None, :]
    allowed = (key_positions[None, :] <= query_positions[:, None]) | (key_positions[None, :] < query_bound[:, None])
    return same_doc & allowed & inside[None, :]

def block_grads(query_rows, key_block, value_block, grad_rows, visible):
    scaling = 1.0 / jnp.sqrt(jnp.float32(key_block.shape[1]))
    query_f = query_rows.astype(jnp.float32)
    key_f = key_block.astype(jnp.float32)
    grad_f = grad_rows.astype(jnp.float32)
    scores = jnp.einsum('thd,kd->htk', query_f, key_f) * scaling
    scores = jnp.where(visible[None], scores, NEGATIVE)
    peak = lax.optimization_barrier(jnp.max(scores, axis=2, keepdims=True))
    expos = jnp.exp(scores - peak)
    attention = expos / lax.optimization_barrier(jnp.sum(expos, axis=2, keepdims=True))
    rounded = attention.astype(jnp.bfloat16)
    grad_probs = jnp.einsum('thd,kd->htk', grad_f, value_block.astype(jnp.float32))
    delta = lax.optimization_barrier(jnp.sum(attention * grad_probs, axis=2, keepdims=True))
    grad_scores = (attention * (grad_probs - delta) * scaling).astype(jnp.bfloat16)
    scores_f = grad_scores.astype(jnp.float32)
    grad_query = jnp.einsum('htk,kd->thd', scores_f, key_f)
    grad_key = jnp.einsum('htk,thd->kd', scores_f, query_f)
    grad_value = jnp.einsum('htk,thd->kd', rounded.astype(jnp.float32), grad_f)
    return (grad_query, grad_key, grad_value)

def reference(layer_input, w_value, queries, keys, grad_out, doc_lengths, prefix_spans):
    value_rows = jnp.dot(layer_input, w_value, preferred_element_type=jnp.float32).astype(jnp.bfloat16)
    ends, prefix_end = doc_tables(doc_lengths, prefix_spans)
    reach = SPAN * TOK_DEV
    window_rows = (2 * SPAN + 1) * TOK_DEV
    padding = jnp.zeros((reach, HD), jnp.bfloat16)
    key_padded = jnp.concatenate([padding, keys, padding], axis=0)
    value_padded = jnp.concatenate([padding, value_rows, padding], axis=0)

    def step(carry, block_index):
        first = block_index * TOK_DEV
        query_rows = lax.dynamic_slice_in_dim(queries, first, TOK_DEV, 0).reshape(TOK_DEV, GROUP, HD)
        grad_rows = lax.dynamic_slice_in_dim(grad_out, first, TOK_DEV, 0).reshape(TOK_DEV, GROUP, HD)
        key_block = lax.dynamic_slice_in_dim(key_padded, first, window_rows, 0)
        value_block = lax.dynamic_slice_in_dim(value_padded, first, window_rows, 0)
        query_positions = (first + jnp.arange(TOK_DEV, dtype=jnp.int32)).astype(jnp.int32)
        key_positions = (first - reach + jnp.arange(window_rows, dtype=jnp.int32)).astype(jnp.int32)
        visible = visible_mask(query_positions, key_positions, ends, prefix_end, TOKENS)
        grad_query, grad_key, grad_value = block_grads(query_rows, key_block, value_block, grad_rows, visible)
        current = lax.dynamic_slice_in_dim(carry, first, window_rows, 0)
        carry = lax.dynamic_update_slice_in_dim(carry, current + jnp.concatenate([grad_key, grad_value], axis=1), first, 0)
        return (carry, grad_query.reshape(TOK_DEV, GROUP * HD).astype(jnp.bfloat16))
    start_carry = jnp.zeros((TOKENS + 2 * reach, 2 * HD), jnp.float32)
    carry, grad_blocks = lax.scan(step, start_carry, jnp.arange(N_DP, dtype=jnp.int32))
    summed = carry[reach:reach + TOKENS]
    grad_keys = summed[:, :HD].astype(jnp.bfloat16)
    grad_value = summed[:, HD:].astype(jnp.bfloat16)
    grad_input = jnp.dot(grad_value, w_value.T, preferred_element_type=jnp.float32).astype(jnp.bfloat16)
    grad_weight = jnp.dot(layer_input.T, grad_value, preferred_element_type=jnp.float32)
    grad_queries = grad_blocks.reshape(TOKENS, GROUP * HD)
    return (grad_input, grad_queries, grad_keys, grad_weight)
```

```python
import math

import jax
import jax.numpy as jnp
from jax import lax
from jax.experimental import pallas as pl
from jax.experimental.pallas import tpu as pltpu
from jax.sharding import PartitionSpec as P

SPAN = 3
NEGATIVE = -1e30
CHUNK = 256
ROWS = 128
BOTH = ("dp", "fsdp")
F32 = jnp.float32
BF16 = jnp.bfloat16
VMEM = pl.BlockSpec(memory_space=pltpu.VMEM)
SMEM = pl.BlockSpec(memory_space=pltpu.SMEM)


def core_swap(value):
    return lax.ppermute(value, "fsdp", [(0, 1), (1, 0)])


def dp_swap(value, mask):
    count = lax.axis_size("dp")
    return lax.ppermute(value, "dp", [(i, i ^ mask) for i in range(count)])


def fan_out(value, distance):
    count = lax.axis_size("dp")
    pairs = [(2 * i, 2 * (i + distance)) for i in range(count - distance)]
    pairs += [(2 * i + 1, 2 * (i - distance) + 1) for i in range(distance, count)]
    return lax.ppermute(value, BOTH, pairs)


def fan_back(value, distance):
    count = lax.axis_size("dp")
    pairs = [(2 * i, 2 * (i - distance)) for i in range(distance, count)]
    pairs += [(2 * i + 1, 2 * (i + distance) + 1) for i in range(count - distance)]
    return lax.ppermute(value, BOTH, pairs)


def chunk_range(first, window_first, lengths_ref, spans_ref, rows_too):
    last = first + ROWS - 1
    zero = jnp.int32(0)
    if rows_too:
        position = first + lax.broadcasted_iota(jnp.int32, (ROWS, 128), 0)
        low, high = jnp.zeros((ROWS, 128), jnp.int32), jnp.zeros((ROWS, 128), jnp.int32)
    else:
        position, low, high = zero, zero, zero

    def step(doc, carry):
        start, least, most, low, high = carry
        length = lengths_ref[doc]
        end = start + length
        bound = start + jnp.minimum(spans_ref[doc], length)
        least = jnp.where((start <= first) & (first < end), start, least)
        most = jnp.where((start <= last) & (last < end), jnp.maximum(last + 1, bound), most)
        if rows_too:
            inside = (position >= start) & (position < end)
            low = jnp.where(inside, start, low)
            high = jnp.where(inside, jnp.maximum(position + 1, bound), high)
        return (end, least, most, low, high)

    carry = (zero, zero, zero, low, high)
    count = lengths_ref.shape[0]
    if count <= 8:
        for doc in range(count):
            carry = step(doc, carry)
    else:
        carry = lax.fori_loop(0, count, step, carry)
    _, least, most, low, high = carry
    chunk_low = lax.div(least - window_first, CHUNK)
    chunk_high = lax.div(most - window_first + CHUNK - 1, CHUNK)
    return chunk_low, chunk_high, low, high


def place_window(core, window_ref, own_ref, mine, other):
    rows = own_ref.shape[0]
    window_ref[SPAN * rows : (SPAN + 1) * rows, :] = own_ref[...]

    def fill(behind, ahead):
        for k in range(1, SPAN + 1):
            window_ref[(SPAN - k) * rows : (SPAN - k + 1) * rows, :] = behind[k - 1][...]
            window_ref[(SPAN + k) * rows : (SPAN + k + 1) * rows, :] = ahead[k - 1][...]

    @pl.when(core == 0)
    def _():
        fill(mine, other)

    @pl.when(core == 1)
    def _():
        fill(other, mine)


def give_out(core, total_ref, own_ref, mine_ref, give_ref, factor):
    rows = own_ref.shape[0]

    def block(index):
        return total_ref[index * rows : (index + 1) * rows, :] * factor

    own_ref[...] = block(SPAN)
    for k in range(1, SPAN + 1):

        @pl.when(core == 0)
        def _():
            mine_ref[k - 1] = block(SPAN - k)
            give_ref[k - 1] = block(SPAN + k)

        @pl.when(core == 1)
        def _():
            mine_ref[k - 1] = block(SPAN + k)
            give_ref[k - 1] = block(SPAN - k)


def stack_heads(ref, first, out_ref):
    for h in range(ref.shape[1] // 128):
        out_ref[h * ROWS : (h + 1) * ROWS, :] = ref[first : first + ROWS, h * 128 : (h + 1) * 128]


def nt_dot(a, b):
    return lax.dot_general(a, b, (((1,), (1,)), ((), ())), preferred_element_type=F32)


def tn_dot(a, b):
    return lax.dot_general(a, b, (((0,), (0,)), ((), ())), preferred_element_type=F32)


def weights_kernel(
    place_ref, lengths_ref, spans_ref, q_ref, grad_ref, key_ref, r1, r2, r3, s1, s2, s3,
    probs_ref, scaled_ref, inverse_ref, window_ref, own_ref, mine_ref, give_ref,
    score_ref, peak_ref, sum_ref, stack_ref, total_ref,
):
    rows = key_ref.shape[0]
    heads = q_ref.shape[1] // 128
    me, core = place_ref[0], place_ref[1]
    place_window(core, window_ref, key_ref, (r1, r2, r3), (s1, s2, s3))
    total_ref[...] = jnp.zeros_like(total_ref)
    window_first = (me - SPAN) * rows
    lane = lax.broadcasted_iota(jnp.int32, (ROWS, 128), 1)
    power = math.log2(math.e) / math.sqrt(128.0)
    for part in range(rows // ROWS):
        stack_heads(q_ref, part * ROWS, stack_ref)
        chunk_low, chunk_high, low, high = chunk_range(
            me * rows + part * ROWS, window_first, lengths_ref, spans_ref, True
        )
        low = low - lane
        high = high - lane
        peak_ref[...] = jnp.full_like(peak_ref, NEGATIVE)
        sum_ref[...] = jnp.zeros_like(sum_ref)

        def score_step(chunk, _):
            keys = window_ref[pl.ds(pl.multiple_of(chunk * CHUNK, CHUNK), CHUNK), :]
            scores = nt_dot(stack_ref[...], keys).reshape(heads, ROWS, CHUNK)
            peak = peak_ref[...]
            for half in range(CHUNK // 128):
                base = window_first + chunk * CHUNK + half * 128
                seen = (low <= base) & (base < high)
                masked = jnp.where(seen[None], scores[:, :, half * 128 : (half + 1) * 128], NEGATIVE)
                score_ref[chunk, :, :, half * 128 : (half + 1) * 128] = masked
                peak = jnp.maximum(peak, masked)
            peak_ref[...] = peak
            return 0

        lax.fori_loop(chunk_low, chunk_high, score_step, 0)
        peak = jnp.max(peak_ref[...], axis=2, keepdims=True)
        peak_ref[...] = jnp.broadcast_to(peak, peak_ref.shape)

        def exp_step(chunk, _):
            total = sum_ref[...]
            peak = peak_ref[...]
            for half in range(CHUNK // 128):
                cut = slice(half * 128, (half + 1) * 128)
                probs = jnp.exp2((score_ref[chunk, :, :, cut] - peak) * power)
                total = total + probs
                probs_ref[part, chunk, :, cut] = probs.reshape(heads * ROWS, 128).astype(BF16)
            sum_ref[...] = total
            return 0

        lax.fori_loop(chunk_low, chunk_high, exp_step, 0)
        inverse = 1.0 / jnp.sum(sum_ref[...], axis=2, keepdims=True)
        inverse_ref[part] = jnp.broadcast_to(inverse, sum_ref.shape).reshape(heads * ROWS, 128)
        for h in range(heads):
            grads = grad_ref[part * ROWS : (part + 1) * ROWS, h * 128 : (h + 1) * 128]
            scaled_ref[part, h * ROWS : (h + 1) * ROWS, :] = (
                grads.astype(F32) * inverse[h]
            ).astype(BF16)

        def value_step(chunk, _):
            at = pl.ds(pl.multiple_of(chunk * CHUNK, CHUNK), CHUNK)
            total_ref[at, :] += tn_dot(probs_ref[part, chunk], scaled_ref[part])
            return 0

        lax.fori_loop(chunk_low, chunk_high, value_step, 0)
    give_out(core, total_ref, own_ref, mine_ref, give_ref, 1.0)


def scores_kernel(
    place_ref, lengths_ref, spans_ref, q_ref, scaled_ref, inverse_ref, probs_ref, keys_ref, value_ref,
    r1, r2, r3, s1, s2, s3,
    grad_q_ref, own_ref, mine_ref, give_ref,
    values_ref, product_ref, delta_ref, stack_ref, query_ref, total_ref,
):
    rows = value_ref.shape[0]
    heads = q_ref.shape[1] // 128
    me, core = place_ref[0], place_ref[1]
    place_window(core, values_ref, value_ref, (r1, r2, r3), (s1, s2, s3))
    total_ref[...] = jnp.zeros_like(total_ref)
    window_first = (me - SPAN) * rows
    scaling = 1.0 / math.sqrt(128.0)
    for part in range(rows // ROWS):
        stack_heads(q_ref, part * ROWS, stack_ref)
        chunk_low, chunk_high, _, _ = chunk_range(
            me * rows + part * ROWS, window_first, lengths_ref, spans_ref, False
        )
        delta_ref[...] = jnp.zeros_like(delta_ref)
        query_ref[...] = jnp.zeros_like(query_ref)

        def delta_step(chunk, _):
            at = pl.ds(pl.multiple_of(chunk * CHUNK, CHUNK), CHUNK)
            product = nt_dot(scaled_ref[part], values_ref[at, :])
            product_ref[chunk] = product
            terms = product * probs_ref[part, chunk].astype(F32)
            delta = delta_ref[...]
            for half in range(CHUNK // 128):
                delta = delta + terms[:, half * 128 : (half + 1) * 128]
            delta_ref[...] = delta
            return 0

        lax.fori_loop(chunk_low, chunk_high, delta_step, 0)
        delta = jnp.sum(delta_ref[...], axis=1, keepdims=True)
        delta_ref[...] = delta * inverse_ref[part]

        def grad_step(chunk, _):
            at = pl.ds(pl.multiple_of(chunk * CHUNK, CHUNK), CHUNK)
            probs = probs_ref[part, chunk].astype(F32)
            delta = delta_ref[...]
            product = product_ref[chunk]
            grad = jnp.concatenate(
                [
                    (probs[:, cut] * (product[:, cut] - delta)).astype(BF16)
                    for cut in (slice(i, i + 128) for i in range(0, CHUNK, 128))
                ],
                axis=1,
            )
            query_ref[...] += jnp.dot(grad, keys_ref[at, :], preferred_element_type=F32)
            total_ref[at, :] += tn_dot(grad, stack_ref[...])
            return 0

        lax.fori_loop(chunk_low, chunk_high, grad_step, 0)
        for h in range(heads):
            grad_q_ref[part * ROWS : (part + 1) * ROWS, h * 128 : (h + 1) * 128] = (
                query_ref[h * ROWS : (h + 1) * ROWS, :] * scaling
            ).astype(BF16)
    give_out(core, total_ref, own_ref, mine_ref, give_ref, scaling)


def value_kernel(place_ref, x_ref, own_ref, z1, z2, z3, other_ref, part_ref, weight_ref):
    me = place_ref[0]
    width = own_ref.shape[0]
    for k, block in enumerate((own_ref, z1, z2, z3)):
        owner = me ^ (2 * k)
        weight_ref[pl.ds(pl.multiple_of(owner * width, width), width), :] = block[...]
        there = owner ^ 1
        weight_ref[pl.ds(pl.multiple_of(there * width, width), width), :] = other_ref[k]
    part_ref[...] = nt_dot(x_ref[...], weight_ref[...])


def weight_grad_kernel(place_ref, a_ref, b_ref, x_ref, grad_ref, keep_ref, send_ref):
    me = place_ref[0]
    grad = (a_ref[...] + b_ref[...]).astype(BF16)
    grad_ref[...] = grad
    depth = x_ref.shape[1]
    width = keep_ref.shape[1]
    step = 512
    for at in range(0, depth, step):
        out = tn_dot(grad, x_ref[:, at : at + step])
        for owner in range(2 * keep_ref.shape[0]):
            rows = out[owner * width : (owner + 1) * width, :]

            @pl.when(lax.rem(me, 2) == owner % 2)
            def _():
                keep_ref[owner // 2, :, at : at + step] = rows

            @pl.when(lax.rem(me, 2) != owner % 2)
            def _():
                send_ref[owner // 2, :, at : at + step] = rows.astype(BF16)


def pair_sum_kernel(place_ref, keep_ref, came_ref, own_ref, z1, z2, z3):
    row = lax.div(place_ref[0], 2)
    own_ref[...] = keep_ref[row] + came_ref[row].astype(F32)
    for k, out in enumerate((z1, z2, z3)):
        there = row ^ (k + 1)
        out[...] = (keep_ref[there] + came_ref[there].astype(F32)).astype(BF16)


def call(kernel, outs, scratch, limit_mib, flops, moved, *args):
    smem = 3 if kernel in (weights_kernel, scores_kernel) else 1
    return pl.pallas_call(
        kernel,
        in_specs=[SMEM] * smem + [VMEM] * (len(args) - smem),
        out_specs=[VMEM] * len(outs),
        out_shape=[jax.ShapeDtypeStruct(shape, kind) for shape, kind in outs],
        scratch_shapes=scratch,
        compiler_params=pltpu.CompilerParams(vmem_limit_bytes=limit_mib << 20),
        cost_estimate=pl.CostEstimate(flops=flops, bytes_accessed=moved, transcendentals=0),
    )(*args)


def returned(own, mine, give):
    got = core_swap(give)
    for k in range(1, SPAN + 1):
        own = own + fan_back((mine[k - 1] + got[k - 1]).astype(BF16), k).astype(F32)
    return own


def body(layer_input, w_value, queries, keys, grad_out, doc_lengths, prefix_spans):
    rows, depth = layer_input.shape
    head = keys.shape[1]
    heads = queries.shape[1] // head
    dp = lax.axis_size("dp")
    window = (2 * SPAN + 1) * rows
    chunks = window // CHUNK
    parts = rows // ROWS
    stack = heads * ROWS
    place = jnp.stack([lax.axis_index("dp"), lax.axis_index("fsdp")]).astype(jnp.int32)
    weight = w_value.T
    width = weight.shape[0]
    direct = dp == 8

    mine = [fan_out(keys, k) for k in range(1, SPAN + 1)]
    other = [core_swap(block) for block in mine]

    if direct:
        columns = [dp_swap(weight, 2 * k) for k in range(1, 4)]
        across = dp_swap(jnp.stack([weight] + columns), 1)

    probs, scaled, inverse, key_window, own, mine_v, give_v = call(
        weights_kernel,
        [
            ((parts, chunks, stack, CHUNK), BF16),
            ((parts, stack, head), BF16),
            ((parts, stack, 128), F32),
            ((window, head), BF16),
            ((rows, head), F32),
            ((SPAN, rows, head), F32),
            ((SPAN, rows, head), F32),
        ],
        [
            pltpu.VMEM((chunks, heads, ROWS, CHUNK), F32),
            pltpu.VMEM((heads, ROWS, 128), F32),
            pltpu.VMEM((heads, ROWS, 128), F32),
            pltpu.VMEM((stack, head), BF16),
            pltpu.VMEM((window, head), F32),
        ],
        24, 1 << 30, 6 << 20,
        place, doc_lengths, prefix_spans, queries, grad_out, keys, *mine, *other,
    )
    half_v = returned(own, mine_v, give_v)
    other_v = core_swap(half_v)

    if direct:
        value_part, full_weight = call(
            value_kernel,
            [((rows, head), F32), ((head, depth), BF16)],
            [], 16, 1 << 28, 4 << 20,
            place, layer_input, weight, *columns, across,
        )
    else:
        full_weight = lax.all_gather(weight, "dp", axis=0, tiled=True)
        value_part = nt_dot(layer_input, full_weight)
    value = (value_part + core_swap(value_part)).astype(BF16)
    mine_x = [fan_out(value, k) for k in range(1, SPAN + 1)]
    other_x = [core_swap(block) for block in mine_x]

    if direct:
        grad_value, keep, send = call(
            weight_grad_kernel,
            [((rows, head), BF16), ((4, width, depth), F32), ((4, width, depth), BF16)],
            [], 16, 1 << 28, 4 << 20,
            place, half_v, other_v, layer_input,
        )
        came = dp_swap(send, 1)
        total, *sends = call(
            pair_sum_kernel,
            [((width, depth), F32)] + [((width, depth), BF16)] * 3,
            [], 16, 1 << 20, 2 << 20,
            place, keep, came,
        )
        for k in range(1, 4):
            total = total + dp_swap(sends[k - 1], 2 * k).astype(F32)
        grad_weight = total.T
    else:
        grad_value = (half_v + other_v).astype(BF16)
        grad_weight = lax.psum_scatter(
            tn_dot(grad_value, layer_input), "dp", scatter_dimension=0, tiled=True
        ).T
    grad_input = jnp.dot(grad_value, full_weight, preferred_element_type=F32).astype(BF16)

    grad_queries, own, mine_k, give_k = call(
        scores_kernel,
        [
            ((rows, heads * head), BF16),
            ((rows, head), F32),
            ((SPAN, rows, head), F32),
            ((SPAN, rows, head), F32),
        ],
        [
            pltpu.VMEM((window, head), BF16),
            pltpu.VMEM((chunks, stack, CHUNK), F32),
            pltpu.VMEM((stack, 128), F32),
            pltpu.VMEM((stack, head), BF16),
            pltpu.VMEM((stack, head), F32),
            pltpu.VMEM((window, head), F32),
        ],
        24, 1 << 30, 6 << 20,
        place, doc_lengths, prefix_spans, queries, scaled, inverse, probs, key_window, value,
        *mine_x, *other_x,
    )
    half_k = returned(own, mine_k, give_k)
    grad_keys = (half_k + core_swap(half_k)).astype(BF16)
    return (grad_input, grad_queries, grad_keys, grad_weight)


def solution(mesh):
    in_specs = (
        P(("groups", "dp"), "fsdp"),
        P("fsdp", "dp"),
        P(("groups", "dp"), "fsdp"),
        P(("groups", "dp"), None),
        P(("groups", "dp"), "fsdp"),
        P("groups"),
        P("groups"),
    )
    out_specs = (
        P(("groups", "dp"), "fsdp"),
        P(("groups", "dp"), "fsdp"),
        P(("groups", "dp"), None),
        P(("groups", "fsdp"), "dp"),
    )
    return jax.shard_map(body, mesh=mesh, in_specs=in_specs, out_specs=out_specs, check_vma=False)
```

```python
import math

import jax
import jax.numpy as jnp
from jax import lax
from jax.experimental import pallas as pl
from jax.experimental.pallas import tpu as pltpu
from jax.sharding import PartitionSpec as P

SPAN = 3
NEGATIVE = -1e30
CHUNK = 256
ROWS = 128
BOTH = ("dp", "fsdp")
F32 = jnp.float32
BF16 = jnp.bfloat16
VMEM = pl.BlockSpec(memory_space=pltpu.VMEM)
SMEM = pl.BlockSpec(memory_space=pltpu.SMEM)


def core_swap(value):
    return lax.ppermute(value, "fsdp", [(0, 1), (1, 0)])


def dp_swap(value, mask):
    count = lax.axis_size("dp")
    return lax.ppermute(value, "dp", [(i, i ^ mask) for i in range(count)])


def fan_out(value, distance):
    count = lax.axis_size("dp")
    pairs = [(2 * i, 2 * (i + distance)) for i in range(count - distance)]
    pairs += [(2 * i + 1, 2 * (i - distance) + 1) for i in range(distance, count)]
    return lax.ppermute(value, BOTH, pairs)


def after(value, *others):
    return lax.optimization_barrier((value, *others))[0]


def chunk_range(first, window_first, lengths_ref, spans_ref, rows_too):
    last = first + ROWS - 1
    zero = jnp.int32(0)
    if rows_too:
        position = first + lax.broadcasted_iota(jnp.int32, (ROWS, 128), 0)
        low, high = jnp.zeros((ROWS, 128), jnp.int32), jnp.zeros((ROWS, 128), jnp.int32)
    else:
        position, low, high = zero, zero, zero

    def step(doc, carry):
        start, least, most, low, high = carry
        length = lengths_ref[doc]
        end = start + length
        bound = start + jnp.minimum(spans_ref[doc], length)
        least = jnp.where((start <= first) & (first < end), start, least)
        most = jnp.where((start <= last) & (last < end), jnp.maximum(last + 1, bound), most)
        if rows_too:
            inside = (position >= start) & (position < end)
            low = jnp.where(inside, start, low)
            high = jnp.where(inside, jnp.maximum(position + 1, bound), high)
        return (end, least, most, low, high)

    carry = (zero, zero, zero, low, high)
    count = lengths_ref.shape[0]
    if count <= 8:
        for doc in range(count):
            carry = step(doc, carry)
    else:
        carry = lax.fori_loop(0, count, step, carry)
    _, least, most, low, high = carry
    chunk_low = lax.div(least - window_first, CHUNK)
    chunk_high = lax.div(most - window_first + CHUNK - 1, CHUNK)
    return chunk_low, chunk_high, low, high


def at_block(index, rows):
    return pl.ds(pl.multiple_of(index * rows, rows), rows)


def place_window(core, window_ref, own, mine, other):
    rows = own.shape[0]
    window_ref[SPAN * rows : (SPAN + 1) * rows, :] = own
    side = 2 * core - 1
    for k in range(1, SPAN + 1):
        window_ref[at_block(SPAN + side * k, rows), :] = mine[k - 1]
        window_ref[at_block(SPAN - side * k, rows), :] = other[k - 1]


def give_out(core, total_ref, own_ref, mine_ref, give_ref, factor):
    rows = own_ref.shape[0]
    own_ref[...] = total_ref[SPAN * rows : (SPAN + 1) * rows, :] * factor
    side = 1 - 2 * core
    for k in range(1, SPAN + 1):
        mine_ref[k - 1] = total_ref[at_block(SPAN + side * k, rows), :] * factor
        give_ref[k - 1] = (total_ref[at_block(SPAN - side * k, rows), :] * factor).astype(BF16)


def stack_heads(ref, first, out_ref):
    for h in range(ref.shape[1] // 128):
        out_ref[h * ROWS : (h + 1) * ROWS, :] = ref[first : first + ROWS, h * 128 : (h + 1) * 128]


def nt_dot(a, b):
    return lax.dot_general(a, b, (((1,), (1,)), ((), ())), preferred_element_type=F32)


def tn_dot(a, b):
    return lax.dot_general(a, b, (((0,), (0,)), ((), ())), preferred_element_type=F32)


def prepare_kernel(
    lengths_ref, spans_ref, q_ref, grad_ref, key_ref,
    range_ref, low_ref, high_ref, queries_ref, grads_ref, own_ref,
):
    rows = key_ref.shape[0]
    me = lax.axis_index("dp")
    window_first = (me - SPAN) * rows
    own_ref[...] = key_ref[...]
    lane = lax.broadcasted_iota(jnp.int32, (ROWS, 128), 1)
    for part in range(rows // ROWS):
        stack_heads(q_ref, part * ROWS, queries_ref.at[part])
        stack_heads(grad_ref, part * ROWS, grads_ref.at[part])
        chunk_low, chunk_high, low, high = chunk_range(
            me * rows + part * ROWS, window_first, lengths_ref, spans_ref, True
        )
        range_ref[2 * part] = chunk_low
        range_ref[2 * part + 1] = chunk_high
        low_ref[part] = low - lane - window_first
        high_ref[part] = high - lane - window_first


def weights_kernel(
    range_ref, low_ref, high_ref, queries_ref, grads_ref, key_ref, r1, r2, r3, s1, s2, s3,
    probs_ref, scaled_ref, inverse_ref, window_ref, own_ref, mine_ref, give_ref,
    score_ref, peak_ref, sum_ref, total_ref,
):
    rows = key_ref.shape[0]
    heads = peak_ref.shape[0]
    core = lax.axis_index("fsdp")
    place_window(
        core, window_ref, key_ref[...], (r1[...], r2[...], r3[...]), (s1[...], s2[...], s3[...])
    )
    total_ref[...] = jnp.zeros_like(total_ref)
    power = math.log2(math.e) / math.sqrt(128.0)
    for part in range(rows // ROWS):
        chunk_low, chunk_high = range_ref[2 * part], range_ref[2 * part + 1]
        low, high = low_ref[part], high_ref[part]
        peak_ref[...] = jnp.full_like(peak_ref, NEGATIVE)
        sum_ref[...] = jnp.zeros_like(sum_ref)

        def score_step(chunk, _):
            keys = window_ref[pl.ds(pl.multiple_of(chunk * CHUNK, CHUNK), CHUNK), :]
            scores = nt_dot(queries_ref[part], keys).reshape(heads, ROWS, CHUNK)
            peak = peak_ref[...]
            for half in range(CHUNK // 128):
                base = chunk * CHUNK + half * 128
                seen = (low <= base) & (base < high)
                masked = jnp.where(seen[None], scores[:, :, half * 128 : (half + 1) * 128], NEGATIVE)
                score_ref[chunk, :, :, half * 128 : (half + 1) * 128] = masked
                peak = jnp.maximum(peak, masked)
            peak_ref[...] = peak
            return 0

        lax.fori_loop(chunk_low, chunk_high, score_step, 0)
        peak = jnp.max(peak_ref[...], axis=2, keepdims=True)
        peak_ref[...] = jnp.broadcast_to(peak, peak_ref.shape)

        def exp_step(chunk, _):
            total = sum_ref[...]
            peak = peak_ref[...]
            for half in range(CHUNK // 128):
                cut = slice(half * 128, (half + 1) * 128)
                probs = jnp.exp2((score_ref[chunk, :, :, cut] - peak) * power)
                total = total + probs
                probs_ref[part, chunk, :, cut] = probs.reshape(heads * ROWS, 128).astype(BF16)
            sum_ref[...] = total
            return 0

        lax.fori_loop(chunk_low, chunk_high, exp_step, 0)
        inverse = 1.0 / jnp.sum(sum_ref[...], axis=2, keepdims=True)
        inverse_ref[part] = jnp.broadcast_to(inverse, sum_ref.shape).reshape(heads * ROWS, 128)
        scaled_ref[part] = (
            (grads_ref[part].astype(F32).reshape(heads, ROWS, 128) * inverse)
            .reshape(heads * ROWS, 128)
            .astype(BF16)
        )

        def value_step(chunk, _):
            at = pl.ds(pl.multiple_of(chunk * CHUNK, CHUNK), CHUNK)
            total_ref[at, :] += tn_dot(probs_ref[part, chunk], scaled_ref[part])
            return 0

        lax.fori_loop(chunk_low, chunk_high, value_step, 0)
    give_out(core, total_ref, own_ref, mine_ref, give_ref, 1.0)


def scores_kernel(
    range_ref, queries_ref, scaled_ref, inverse_ref, probs_ref, keys_ref, value_ref,
    r1, r2, r3, s1, s2, s3,
    grad_q_ref, own_ref, mine_ref, give_ref,
    values_ref, product_ref, delta_ref, query_ref, total_ref,
):
    rows = value_ref.shape[0]
    heads = grad_q_ref.shape[1] // 128
    core = lax.axis_index("fsdp")
    place_window(core, values_ref, value_ref[...], (r1[0], r2[0], r3[0]), (s1[0], s2[0], s3[0]))
    total_ref[...] = jnp.zeros_like(total_ref)
    scaling = 1.0 / math.sqrt(128.0)
    for part in range(rows // ROWS):
        chunk_low, chunk_high = range_ref[2 * part], range_ref[2 * part + 1]
        delta_ref[...] = jnp.zeros_like(delta_ref)
        query_ref[...] = jnp.zeros_like(query_ref)

        def delta_step(chunk, _):
            at = pl.ds(pl.multiple_of(chunk * CHUNK, CHUNK), CHUNK)
            product = nt_dot(scaled_ref[part], values_ref[at, :])
            product_ref[chunk] = product
            terms = product * probs_ref[part, chunk].astype(F32)
            delta = delta_ref[...]
            for half in range(CHUNK // 128):
                delta = delta + terms[:, half * 128 : (half + 1) * 128]
            delta_ref[...] = delta
            return 0

        lax.fori_loop(chunk_low, chunk_high, delta_step, 0)
        delta = jnp.sum(delta_ref[...], axis=1, keepdims=True)
        delta_ref[...] = delta * inverse_ref[part]

        def grad_step(chunk, _):
            at = pl.ds(pl.multiple_of(chunk * CHUNK, CHUNK), CHUNK)
            probs = probs_ref[part, chunk].astype(F32)
            delta = delta_ref[...]
            product = product_ref[chunk]
            grad = jnp.concatenate(
                [
                    (probs[:, cut] * (product[:, cut] - delta)).astype(BF16)
                    for cut in (slice(i, i + 128) for i in range(0, CHUNK, 128))
                ],
                axis=1,
            )
            query_ref[...] += jnp.dot(grad, keys_ref[at, :], preferred_element_type=F32)
            total_ref[at, :] += tn_dot(grad, queries_ref[part])
            return 0

        lax.fori_loop(chunk_low, chunk_high, grad_step, 0)
        for h in range(heads):
            grad_q_ref[part * ROWS : (part + 1) * ROWS, h * 128 : (h + 1) * 128] = (
                query_ref[h * ROWS : (h + 1) * ROWS, :] * scaling
            ).astype(BF16)
    give_out(core, total_ref, own_ref, mine_ref, give_ref, scaling)


def pack_kernel(half_ref, other_ref, mine_ref, got_ref, value_ref, *outs):
    value = (half_ref[...] + other_ref[...]).astype(BF16)
    value_ref[...] = value
    for k, out in enumerate(outs):
        out[0] = value
        out[1] = (mine_ref[k] + got_ref[k].astype(F32)).astype(BF16)


def sum_blocks(own, other, mine, others):
    total = own + other
    for a, b in zip(mine, others):
        total = total + (a.astype(F32) + b.astype(F32))
    return total


def value_kernel(x_ref, z0, z1, z2, z3, c0, c1, c2, c3, part_ref, weight_ref):
    me = lax.axis_index("dp")
    width = z0.shape[0]
    for k, (near, cross) in enumerate(((z0, c0), (z1, c1), (z2, c2), (z3, c3))):
        owner = me ^ (2 * k)
        weight_ref[pl.ds(pl.multiple_of(owner * width, width), width), :] = near[...]
        there = owner ^ 1
        weight_ref[pl.ds(pl.multiple_of(there * width, width), width), :] = cross[...]
    part_ref[...] = nt_dot(x_ref[...], weight_ref[...])


def weight_grad_kernel(x_ref, a_ref, b_ref, r1, r2, r3, s1, s2, s3, grad_ref, *outs):
    me = lax.axis_index("dp")
    grad = sum_blocks(
        a_ref[...], b_ref[...], (r1[1], r2[1], r3[1]), (s1[1], s2[1], s3[1])
    ).astype(BF16)
    grad_ref[...] = grad
    depth = x_ref.shape[1]
    width = outs[0].shape[0]
    step = 512
    scratch = outs[8]
    for at in range(0, depth, step):
        scratch[:, at : at + step] = tn_dot(grad, x_ref[:, at : at + step])
    for k in range(4):
        owner = me ^ (2 * k)
        outs[k][...] = scratch[pl.ds(pl.multiple_of(owner * width, width), width), :]
        there = owner ^ 1
        rows = scratch[pl.ds(pl.multiple_of(there * width, width), width), :]
        outs[4 + k][...] = rows.astype(BF16)


def call(kernel, outs, scratch, limit_mib, smem, *args):
    return pl.pallas_call(
        kernel,
        in_specs=[SMEM] * smem + [VMEM] * (len(args) - smem),
        out_specs=[SMEM if len(shape) == 1 else VMEM for shape, _ in outs],
        out_shape=[jax.ShapeDtypeStruct(shape, kind) for shape, kind in outs],
        scratch_shapes=scratch,
        compiler_params=pltpu.CompilerParams(vmem_limit_bytes=limit_mib << 20),
        cost_estimate=pl.CostEstimate(flops=1 << 30, bytes_accessed=4 << 20, transcendentals=0),
    )(*args)


def body(layer_input, w_value, queries, keys, grad_out, doc_lengths, prefix_spans):
    rows, depth = layer_input.shape
    head = keys.shape[1]
    heads = queries.shape[1] // head
    dp = lax.axis_size("dp")
    window = (2 * SPAN + 1) * rows
    chunks = window // CHUNK
    parts = rows // ROWS
    stack = heads * ROWS
    weight = w_value.T
    width = weight.shape[0]
    direct = dp == 8
    distances = range(1, SPAN + 1)

    first = keys
    if direct:
        z3, z2, z1 = (dp_swap(weight, 2 * k) for k in (3, 2, 1))
        cross0 = dp_swap(weight, 1)
        first = after(keys, cross0)

    ranges, low, high, query_stack, grad_stack, own_keys = call(
        prepare_kernel,
        [
            ((2 * parts,), jnp.int32),
            ((parts, ROWS, 128), jnp.int32),
            ((parts, ROWS, 128), jnp.int32),
            ((parts, stack, head), BF16),
            ((parts, stack, head), BF16),
            ((rows, head), BF16),
        ],
        [], 8, 2,
        doc_lengths, prefix_spans, queries, grad_out, first,
    )
    mine = [fan_out(own_keys, k) for k in distances]
    other = [core_swap(block) for block in mine]

    probs, scaled, inverse, key_window, own_v, mine_v, give_v = call(
        weights_kernel,
        [
            ((parts, chunks, stack, CHUNK), BF16),
            ((parts, stack, head), BF16),
            ((parts, stack, 128), F32),
            ((window, head), BF16),
            ((rows, head), F32),
            ((SPAN, rows, head), F32),
            ((SPAN, rows, head), BF16),
        ],
        [
            pltpu.VMEM((chunks, heads, ROWS, CHUNK), F32),
            pltpu.VMEM((heads, ROWS, 128), F32),
            pltpu.VMEM((heads, ROWS, 128), F32),
            pltpu.VMEM((window, head), F32),
        ],
        20, 1,
        ranges, low, high, query_stack, grad_stack, own_keys, *mine, *other,
    )
    got_v = core_swap(give_v)
    other_v = core_swap(own_v)

    if direct:
        cross = [cross0] + [dp_swap(block, 1) for block in (z1, z2, z3)]
        value_part, full_weight = call(
            value_kernel,
            [((rows, head), F32), ((head, depth), BF16)],
            [], 12, 0,
            layer_input, weight, z1, z2, z3, *cross,
        )
    else:
        full_weight = lax.all_gather(weight, "dp", axis=0, tiled=True)
        value_part = nt_dot(layer_input, full_weight)
    value, *packs = call(
        pack_kernel,
        [((rows, head), BF16)] + [((2, rows, head), BF16)] * SPAN,
        [], 8, 0,
        value_part, core_swap(value_part), mine_v, got_v,
    )
    mine = [fan_out(pack, k) for pack, k in zip(packs, distances)]
    other = [core_swap(block) for block in mine]

    if direct:
        grad_value, *blocks = call(
            weight_grad_kernel,
            [((rows, head), BF16)] + [((width, depth), F32)] * 4 + [((width, depth), BF16)] * 4,
            [pltpu.VMEM((head, depth), F32)], 16, 0,
            layer_input, own_v, other_v, *mine, *other,
        )
        keep, send = blocks[:4], blocks[4:]
        total = keep[0]
        for k in (3, 2, 1):
            pair = (keep[k] + dp_swap(send[k], 1).astype(F32)).astype(BF16)
            total = total + dp_swap(pair, 2 * k).astype(F32)
        total = total + dp_swap(send[0], 1).astype(F32)
        grad_weight = total.T
    else:
        grad_value = sum_blocks(
            own_v, other_v, [block[1] for block in mine], [block[1] for block in other]
        ).astype(BF16)
        grad_weight = lax.psum_scatter(
            tn_dot(grad_value, layer_input), "dp", scatter_dimension=0, tiled=True
        ).T
    grad_input = jnp.dot(grad_value, full_weight, preferred_element_type=F32).astype(BF16)

    grad_queries, own_k, mine_k, give_k = call(
        scores_kernel,
        [
            ((rows, heads * head), BF16),
            ((rows, head), F32),
            ((SPAN, rows, head), F32),
            ((SPAN, rows, head), BF16),
        ],
        [
            pltpu.VMEM((window, head), BF16),
            pltpu.VMEM((chunks, stack, CHUNK), F32),
            pltpu.VMEM((stack, 128), F32),
            pltpu.VMEM((stack, head), F32),
            pltpu.VMEM((window, head), F32),
        ],
        20, 1,
        ranges, query_stack, scaled, inverse, probs, key_window, value, *mine, *other,
    )
    got_k = core_swap(give_k)
    mine = [
        fan_out((mine_k[k - 1] + got_k[k - 1].astype(F32)).astype(BF16), k) for k in distances
    ]
    other = [core_swap(block) for block in mine]
    grad_keys = sum_blocks(own_k, core_swap(own_k), mine, other).astype(BF16)
    return (grad_input, grad_queries, grad_keys, grad_weight)


def solution(mesh):
    in_specs = (
        P(("groups", "dp"), "fsdp"),
        P("fsdp", "dp"),
        P(("groups", "dp"), "fsdp"),
        P(("groups", "dp"), None),
        P(("groups", "dp"), "fsdp"),
        P("groups"),
        P("groups"),
    )
    out_specs = (
        P(("groups", "dp"), "fsdp"),
        P(("groups", "dp"), "fsdp"),
        P(("groups", "dp"), None),
        P(("groups", "fsdp"), "dp"),
    )
    return jax.shard_map(body, mesh=mesh, in_specs=in_specs, out_specs=out_specs, check_vma=False)
```

```python
import math

import jax
import jax.numpy as jnp
from jax import lax
from jax.experimental import pallas as pl
from jax.experimental.pallas import tpu as pltpu
from jax.sharding import PartitionSpec as P

SPAN = 3
NEGATIVE = -1e30
CHUNK = 256
ROWS = 128
BOTH = ("dp", "fsdp")
F32 = jnp.float32
BF16 = jnp.bfloat16
VMEM = pl.BlockSpec(memory_space=pltpu.VMEM)
SMEM = pl.BlockSpec(memory_space=pltpu.SMEM)


def core_swap(value):
    return lax.ppermute(value, "fsdp", [(0, 1), (1, 0)])


def dp_swap(value, mask):
    count = lax.axis_size("dp")
    return lax.ppermute(value, "dp", [(i, i ^ mask) for i in range(count)])


def fan_out(value, distance):
    count = lax.axis_size("dp")
    pairs = [(2 * i, 2 * (i + distance)) for i in range(count - distance)]
    pairs += [(2 * i + 1, 2 * (i - distance) + 1) for i in range(distance, count)]
    return lax.ppermute(value, BOTH, pairs)


def after(value, *others):
    return lax.optimization_barrier((value, *others))[0]


def chunk_range(first, window_first, docs_ref):
    last = first + ROWS - 1
    zero = jnp.int32(0)
    count = docs_ref.shape[0] // 2
    position = first + lax.broadcasted_iota(jnp.int32, (ROWS, 128), 0)
    low, high = jnp.zeros((ROWS, 128), jnp.int32), jnp.zeros((ROWS, 128), jnp.int32)

    def step(doc, carry):
        start, least, most, low, high = carry
        length = docs_ref[doc]
        end = start + length
        bound = start + jnp.minimum(docs_ref[count + doc], length)
        least = jnp.where((start <= first) & (first < end), start, least)
        most = jnp.where((start <= last) & (last < end), jnp.maximum(last + 1, bound), most)
        inside = (position >= start) & (position < end)
        low = jnp.where(inside, start, low)
        high = jnp.where(inside, jnp.maximum(position + 1, bound), high)
        return (end, least, most, low, high)

    carry = (zero, zero, zero, low, high)
    if count <= 8:
        for doc in range(count):
            carry = step(doc, carry)
    else:
        carry = lax.fori_loop(0, count, step, carry)
    _, least, most, low, high = carry
    chunk_low = lax.div(least - window_first, CHUNK)
    chunk_high = lax.div(most - window_first + CHUNK - 1, CHUNK)
    return chunk_low, chunk_high, low, high


def at_block(index, rows):
    return pl.ds(pl.multiple_of(index * rows, rows), rows)


def place_window(core, window_ref, own, mine, other):
    rows = own.shape[0]
    window_ref[SPAN * rows : (SPAN + 1) * rows, :] = own
    side = 2 * core - 1
    for k in range(1, SPAN + 1):
        window_ref[at_block(SPAN + side * k, rows), :] = mine[k - 1]
        window_ref[at_block(SPAN - side * k, rows), :] = other[k - 1]


def give_out(core, total_ref, own_ref, mine_ref, give_ref, factor):
    rows = own_ref.shape[0]
    own_ref[...] = total_ref[SPAN * rows : (SPAN + 1) * rows, :] * factor
    side = 1 - 2 * core
    for k in range(1, SPAN + 1):
        mine_ref[k - 1] = total_ref[at_block(SPAN + side * k, rows), :] * factor
        give_ref[k - 1] = (total_ref[at_block(SPAN - side * k, rows), :] * factor).astype(BF16)


def stack_heads(value, head):
    rows, wide = value.shape
    split = value.reshape(rows // ROWS, ROWS, wide // head, head)
    return split.transpose(0, 2, 1, 3).reshape(rows // ROWS, -1, head)


def nt_dot(a, b):
    return lax.dot_general(a, b, (((1,), (1,)), ((), ())), preferred_element_type=F32)


def tn_dot(a, b):
    return lax.dot_general(a, b, (((0,), (0,)), ((), ())), preferred_element_type=F32)


def weights_kernel(
    docs_ref, queries_ref, grads_ref, key_ref, r1, r2, r3, s1, s2, s3,
    range_ref, probs_ref, scaled_ref, inverse_ref, window_ref, own_ref, mine_ref, give_ref,
    score_ref, peak_ref, sum_ref, total_ref,
):
    rows = key_ref.shape[0]
    heads = peak_ref.shape[0]
    me, core = lax.axis_index("dp"), lax.axis_index("fsdp")
    window_first = (me - SPAN) * rows
    lane = lax.broadcasted_iota(jnp.int32, (ROWS, 128), 1)
    place_window(
        core, window_ref, key_ref[...], (r1[...], r2[...], r3[...]), (s1[...], s2[...], s3[...])
    )
    total_ref[...] = jnp.zeros_like(total_ref)
    power = math.log2(math.e) / math.sqrt(128.0)
    for part in range(rows // ROWS):
        chunk_low, chunk_high, low, high = chunk_range(
            me * rows + part * ROWS, window_first, docs_ref
        )
        range_ref[2 * part] = chunk_low
        range_ref[2 * part + 1] = chunk_high
        low = low - lane - window_first
        high = high - lane - window_first
        peak_ref[...] = jnp.full_like(peak_ref, NEGATIVE)
        sum_ref[...] = jnp.zeros_like(sum_ref)

        def score_step(chunk, _):
            keys = window_ref[pl.ds(pl.multiple_of(chunk * CHUNK, CHUNK), CHUNK), :]
            scores = nt_dot(queries_ref[part], keys).reshape(heads, ROWS, CHUNK)
            peak = peak_ref[...]
            for half in range(CHUNK // 128):
                base = chunk * CHUNK + half * 128
                seen = (low <= base) & (base < high)
                masked = jnp.where(seen[None], scores[:, :, half * 128 : (half + 1) * 128], NEGATIVE)
                score_ref[chunk, :, :, half * 128 : (half + 1) * 128] = masked
                peak = jnp.maximum(peak, masked)
            peak_ref[...] = peak
            return 0

        lax.fori_loop(chunk_low, chunk_high, score_step, 0)
        peak = jnp.max(peak_ref[...], axis=2, keepdims=True)
        peak_ref[...] = jnp.broadcast_to(peak, peak_ref.shape)

        def exp_step(chunk, _):
            total = sum_ref[...]
            peak = peak_ref[...]
            for half in range(CHUNK // 128):
                cut = slice(half * 128, (half + 1) * 128)
                probs = jnp.exp2((score_ref[chunk, :, :, cut] - peak) * power)
                total = total + probs
                probs_ref[part, chunk, :, cut] = probs.reshape(heads * ROWS, 128).astype(BF16)
            sum_ref[...] = total
            return 0

        lax.fori_loop(chunk_low, chunk_high, exp_step, 0)
        inverse = 1.0 / jnp.sum(sum_ref[...], axis=2, keepdims=True)
        inverse_ref[part] = jnp.broadcast_to(inverse, sum_ref.shape).reshape(heads * ROWS, 128)
        scaled_ref[part] = (
            (grads_ref[part].astype(F32).reshape(heads, ROWS, 128) * inverse)
            .reshape(heads * ROWS, 128)
            .astype(BF16)
        )

        def value_step(chunk, _):
            at = pl.ds(pl.multiple_of(chunk * CHUNK, CHUNK), CHUNK)
            total_ref[at, :] += tn_dot(probs_ref[part, chunk], scaled_ref[part])
            return 0

        lax.fori_loop(chunk_low, chunk_high, value_step, 0)
    give_out(core, total_ref, own_ref, mine_ref, give_ref, 1.0)


def scores_kernel(
    range_ref, queries_ref, scaled_ref, inverse_ref, probs_ref, keys_ref, value_ref,
    r1, r2, r3, s1, s2, s3,
    grad_q_ref, own_ref, mine_ref, give_ref,
    values_ref, product_ref, delta_ref, query_ref, total_ref,
):
    rows = value_ref.shape[0]
    heads = grad_q_ref.shape[1] // 128
    core = lax.axis_index("fsdp")
    place_window(core, values_ref, value_ref[...], (r1[0], r2[0], r3[0]), (s1[0], s2[0], s3[0]))
    total_ref[...] = jnp.zeros_like(total_ref)
    scaling = 1.0 / math.sqrt(128.0)
    for part in range(rows // ROWS):
        chunk_low, chunk_high = range_ref[2 * part], range_ref[2 * part + 1]
        delta_ref[...] = jnp.zeros_like(delta_ref)
        query_ref[...] = jnp.zeros_like(query_ref)

        def delta_step(chunk, _):
            at = pl.ds(pl.multiple_of(chunk * CHUNK, CHUNK), CHUNK)
            product = nt_dot(scaled_ref[part], values_ref[at, :])
            product_ref[chunk] = product
            terms = product * probs_ref[part, chunk].astype(F32)
            delta = delta_ref[...]
            for half in range(CHUNK // 128):
                delta = delta + terms[:, half * 128 : (half + 1) * 128]
            delta_ref[...] = delta
            return 0

        lax.fori_loop(chunk_low, chunk_high, delta_step, 0)
        delta = jnp.sum(delta_ref[...], axis=1, keepdims=True)
        delta_ref[...] = delta * inverse_ref[part]

        def grad_step(chunk, _):
            at = pl.ds(pl.multiple_of(chunk * CHUNK, CHUNK), CHUNK)
            probs = probs_ref[part, chunk].astype(F32)
            delta = delta_ref[...]
            product = product_ref[chunk]
            grad = jnp.concatenate(
                [
                    (probs[:, cut] * (product[:, cut] - delta)).astype(BF16)
                    for cut in (slice(i, i + 128) for i in range(0, CHUNK, 128))
                ],
                axis=1,
            )
            query_ref[...] += jnp.dot(grad, keys_ref[at, :], preferred_element_type=F32)
            total_ref[at, :] += tn_dot(grad, queries_ref[part])
            return 0

        lax.fori_loop(chunk_low, chunk_high, grad_step, 0)
        for h in range(heads):
            grad_q_ref[part * ROWS : (part + 1) * ROWS, h * 128 : (h + 1) * 128] = (
                query_ref[h * ROWS : (h + 1) * ROWS, :] * scaling
            ).astype(BF16)
    give_out(core, total_ref, own_ref, mine_ref, give_ref, scaling)


def pack_kernel(half_ref, other_ref, mine_ref, got_ref, value_ref, *outs):
    value = (half_ref[...] + other_ref[...]).astype(BF16)
    value_ref[...] = value
    for k, out in enumerate(outs):
        out[0] = value
        out[1] = (mine_ref[k] + got_ref[k].astype(F32)).astype(BF16)


def sum_blocks(own, other, mine, others):
    total = own + other
    for a, b in zip(mine, others):
        total = total + (a.astype(F32) + b.astype(F32))
    return total


def value_kernel(x_ref, z0, z1, z2, z3, c0, c1, c2, c3, part_ref, weight_ref):
    me = lax.axis_index("dp")
    width = z0.shape[0]
    for k, (near, cross) in enumerate(((z0, c0), (z1, c1), (z2, c2), (z3, c3))):
        owner = me ^ (2 * k)
        weight_ref[pl.ds(pl.multiple_of(owner * width, width), width), :] = near[...]
        there = owner ^ 1
        weight_ref[pl.ds(pl.multiple_of(there * width, width), width), :] = cross[...]
    part_ref[...] = nt_dot(x_ref[...], weight_ref[...])


def weight_grad_kernel(x_ref, a_ref, b_ref, r1, r2, r3, s1, s2, s3, grad_ref, *outs):
    me = lax.axis_index("dp")
    grad = sum_blocks(
        a_ref[...], b_ref[...], (r1[1], r2[1], r3[1]), (s1[1], s2[1], s3[1])
    ).astype(BF16)
    grad_ref[...] = grad
    depth = x_ref.shape[1]
    width = outs[0].shape[0]
    step = 512
    scratch = outs[8]
    for at in range(0, depth, step):
        scratch[:, at : at + step] = tn_dot(grad, x_ref[:, at : at + step])
    for k in range(4):
        owner = me ^ (2 * k)
        outs[k][...] = scratch[pl.ds(pl.multiple_of(owner * width, width), width), :]
        there = owner ^ 1
        rows = scratch[pl.ds(pl.multiple_of(there * width, width), width), :]
        outs[4 + k][...] = rows.astype(BF16)


def call(kernel, outs, scratch, limit_mib, smem, *args):
    return pl.pallas_call(
        kernel,
        in_specs=[SMEM] * smem + [VMEM] * (len(args) - smem),
        out_specs=[SMEM if len(shape) == 1 else VMEM for shape, _ in outs],
        out_shape=[jax.ShapeDtypeStruct(shape, kind) for shape, kind in outs],
        scratch_shapes=scratch,
        compiler_params=pltpu.CompilerParams(vmem_limit_bytes=limit_mib << 20),
        cost_estimate=pl.CostEstimate(flops=1 << 30, bytes_accessed=4 << 20, transcendentals=0),
    )(*args)


def body(layer_input, w_value, queries, keys, grad_out, doc_lengths, prefix_spans):
    rows, depth = layer_input.shape
    head = keys.shape[1]
    heads = queries.shape[1] // head
    dp = lax.axis_size("dp")
    window = (2 * SPAN + 1) * rows
    chunks = window // CHUNK
    parts = rows // ROWS
    stack = heads * ROWS
    weight = w_value.T
    width = weight.shape[0]
    direct = dp == 8
    distances = range(1, SPAN + 1)

    mine = [fan_out(keys, k) for k in distances]
    other = [core_swap(block) for block in mine]
    if direct:
        weight = after(weight, mine[0])
        z3, z2, z1 = (dp_swap(weight, 2 * k) for k in (3, 2, 1))
        cross0 = dp_swap(weight, 1)

    query_stack = stack_heads(queries, head)
    grad_stack = stack_heads(grad_out, head)

    ranges, probs, scaled, inverse, key_window, own_v, mine_v, give_v = call(
        weights_kernel,
        [
            ((2 * parts,), jnp.int32),
            ((parts, chunks, stack, CHUNK), BF16),
            ((parts, stack, head), BF16),
            ((parts, stack, 128), F32),
            ((window, head), BF16),
            ((rows, head), F32),
            ((SPAN, rows, head), F32),
            ((SPAN, rows, head), BF16),
        ],
        [
            pltpu.VMEM((chunks, heads, ROWS, CHUNK), F32),
            pltpu.VMEM((heads, ROWS, 128), F32),
            pltpu.VMEM((heads, ROWS, 128), F32),
            pltpu.VMEM((window, head), F32),
        ],
        20, 1,
        jnp.concatenate([doc_lengths, prefix_spans]), query_stack, grad_stack, keys, *mine, *other,
    )
    got_v = core_swap(give_v)
    other_v = core_swap(own_v)

    if direct:
        cross = [cross0] + [dp_swap(block, 1) for block in (z1, z2, z3)]
        value_part, full_weight = call(
            value_kernel,
            [((rows, head), F32), ((head, depth), BF16)],
            [], 12, 0,
            layer_input, weight, z1, z2, z3, *cross,
        )
    else:
        full_weight = lax.all_gather(weight, "dp", axis=0, tiled=True)
        value_part = nt_dot(layer_input, full_weight)
    value, *packs = call(
        pack_kernel,
        [((rows, head), BF16)] + [((2, rows, head), BF16)] * SPAN,
        [], 8, 0,
        value_part, core_swap(value_part), mine_v, got_v,
    )
    mine = [fan_out(pack, k) for pack, k in zip(packs, distances)]
    other = [core_swap(block) for block in mine]

    if direct:
        grad_value, *blocks = call(
            weight_grad_kernel,
            [((rows, head), BF16)] + [((width, depth), F32)] * 4 + [((width, depth), BF16)] * 4,
            [pltpu.VMEM((head, depth), F32)], 16, 0,
            layer_input, own_v, other_v, *mine, *other,
        )
        keep, send = blocks[:4], blocks[4:]
        total = keep[0]
        for k in (3, 2, 1):
            pair = (keep[k] + dp_swap(send[k], 1).astype(F32)).astype(BF16)
            total = total + dp_swap(pair, 2 * k).astype(F32)
        total = total + dp_swap(send[0], 1).astype(F32)
        grad_weight = total.T
    else:
        grad_value = sum_blocks(
            own_v, other_v, [block[1] for block in mine], [block[1] for block in other]
        ).astype(BF16)
        grad_weight = lax.psum_scatter(
            tn_dot(grad_value, layer_input), "dp", scatter_dimension=0, tiled=True
        ).T
    grad_queries, own_k, mine_k, give_k = call(
        scores_kernel,
        [
            ((rows, heads * head), BF16),
            ((rows, head), F32),
            ((SPAN, rows, head), F32),
            ((SPAN, rows, head), BF16),
        ],
        [
            pltpu.VMEM((window, head), BF16),
            pltpu.VMEM((chunks, stack, CHUNK), F32),
            pltpu.VMEM((stack, 128), F32),
            pltpu.VMEM((stack, head), F32),
            pltpu.VMEM((window, head), F32),
        ],
        20, 1,
        after(ranges, grad_value), query_stack, scaled, inverse, probs, key_window, value, *mine, *other,
    )
    got_k = core_swap(give_k)
    mine = [
        fan_out((mine_k[k - 1] + got_k[k - 1].astype(F32)).astype(BF16), k) for k in distances
    ]
    other = [core_swap(block) for block in mine]
    grad_input = jnp.dot(
        grad_value, full_weight, preferred_element_type=F32
    ).astype(BF16)
    grad_keys = sum_blocks(own_k, core_swap(own_k), mine, other).astype(BF16)
    return (grad_input, grad_queries, grad_keys, grad_weight)


def solution(mesh):
    in_specs = (
        P(("groups", "dp"), "fsdp"),
        P("fsdp", "dp"),
        P(("groups", "dp"), "fsdp"),
        P(("groups", "dp"), None),
        P(("groups", "dp"), "fsdp"),
        P("groups"),
        P("groups"),
    )
    out_specs = (
        P(("groups", "dp"), "fsdp"),
        P(("groups", "dp"), "fsdp"),
        P(("groups", "dp"), None),
        P(("groups", "fsdp"), "dp"),
    )
    return jax.shard_map(body, mesh=mesh, in_specs=in_specs, out_specs=out_specs, check_vma=False)
```

```python
import math

import jax
import jax.numpy as jnp
from jax import lax
from jax.experimental import pallas as pl
from jax.experimental.pallas import tpu as pltpu
from jax.sharding import PartitionSpec as P

SPAN = 3
NEGATIVE = -1e30
CHUNK = 256
ROWS = 128
BOTH = ("dp", "fsdp")
F32 = jnp.float32
BF16 = jnp.bfloat16
VMEM = pl.BlockSpec(memory_space=pltpu.VMEM)
SMEM = pl.BlockSpec(memory_space=pltpu.SMEM)


def core_swap(value):
    return lax.ppermute(value, "fsdp", [(0, 1), (1, 0)])


def dp_swap(value, mask):
    count = lax.axis_size("dp")
    return lax.ppermute(value, "dp", [(i, i ^ mask) for i in range(count)])


def reach(step, core, odd):
    turn = 1 - 2 * odd
    return ((-3 * turn, turn - 2), (-2, turn + 2), (2, turn))[step][core]


def offset(step, core, odd, sign):
    turn = 1 - 2 * odd
    near = ((0, -2), (-2, 2), (2, 0))[step]
    first = -3 * turn if step == 0 else sign * near[0]
    return jnp.where(core == 0, first, sign * near[1] + turn)


def fan_out(value, step):
    count = lax.axis_size("dp")
    pairs = [(2 * i + c, 2 * (i + reach(step, c, i % 2)) + c) for i in range(count) for c in (0, 1)]
    return lax.ppermute(value, BOTH, [(i, j) for i, j in pairs if 0 <= j < 2 * count])


def after(value, *others):
    return lax.optimization_barrier((value, *others))[0]


def chunk_range(first, window_first, docs_ref):
    last = first + ROWS - 1
    zero = jnp.int32(0)
    count = docs_ref.shape[0] // 2
    position = first + lax.broadcasted_iota(jnp.int32, (1, ROWS), 1)
    low, high = jnp.zeros((1, ROWS), jnp.int32), jnp.zeros((1, ROWS), jnp.int32)

    def step(doc, carry):
        start, least, most, low, high = carry
        length = docs_ref[doc]
        end = start + length
        bound = start + jnp.minimum(docs_ref[count + doc], length)
        least = jnp.where((start <= first) & (first < end), start, least)
        most = jnp.where((start <= last) & (last < end), jnp.maximum(last + 1, bound), most)
        inside = (position >= start) & (position < end)
        low = jnp.where(inside, start, low)
        high = jnp.where(inside, jnp.maximum(position + 1, bound), high)
        return (end, least, most, low, high)

    carry = (zero, zero, zero, low, high)
    if count <= 8:
        for doc in range(count):
            carry = step(doc, carry)
    else:
        carry = lax.fori_loop(0, count, step, carry)
    _, least, most, low, high = carry
    chunk_low = lax.div(least - window_first, CHUNK)
    chunk_high = lax.div(most - window_first + CHUNK - 1, CHUNK)
    return chunk_low, chunk_high, low, high


def at_block(index, rows):
    return pl.ds(pl.multiple_of(index * rows, rows), rows)


def place_window(core, window_ref, own, mine, other):
    rows = own.shape[0]
    odd = lax.rem(lax.axis_index("dp"), 2)
    window_ref[SPAN * rows : (SPAN + 1) * rows, :] = own
    for k in range(SPAN):
        window_ref[at_block(SPAN + offset(k, core, odd, -1), rows), :] = mine[k]
        window_ref[at_block(SPAN + offset(k, 1 - core, odd, -1), rows), :] = other[k]


def give_out(core, total_ref, own_ref, mine_ref, give_ref, factor):
    rows = own_ref.shape[0]
    odd = lax.rem(lax.axis_index("dp"), 2)
    own_ref[...] = total_ref[SPAN * rows : (SPAN + 1) * rows, :] * factor
    for k in range(SPAN):
        mine_ref[k] = total_ref[at_block(SPAN + offset(k, core, odd, 1), rows), :] * factor
        there = total_ref[at_block(SPAN + offset(k, 1 - core, odd, 1), rows), :] * factor
        give_ref[k] = there.astype(BF16)


def stack_heads(value, head):
    rows, wide = value.shape
    split = value.reshape(rows // ROWS, ROWS, wide // head, head)
    return split.transpose(0, 2, 1, 3).reshape(rows // ROWS, -1, head)


def nt_dot(a, b):
    return lax.dot_general(a, b, (((1,), (1,)), ((), ())), preferred_element_type=F32)


def tn_dot(a, b):
    return lax.dot_general(a, b, (((0,), (0,)), ((), ())), preferred_element_type=F32)


def fold(total, value, reduce):
    rows, lanes = value.shape
    return reduce(jnp.concatenate([total[None], value.reshape(rows // 8, 8, lanes)]), axis=0)


def weights_kernel(
    docs_ref, queries_ref, grads_ref, key_ref, r1, r2, r3, s1, s2, s3,
    range_ref, probs_ref, window_ref, own_ref, mine_ref, give_ref,
    score_ref, peak_ref, sum_ref, total_ref,
):
    rows = key_ref.shape[0]
    stack = queries_ref.shape[1]
    me, core = lax.axis_index("dp"), lax.axis_index("fsdp")
    window_first = (me - SPAN) * rows
    place_window(
        core, window_ref, key_ref[...], (r1[...], r2[...], r3[...]), (s1[...], s2[...], s3[...])
    )
    total_ref[...] = jnp.zeros_like(total_ref)
    power = math.log2(math.e) / math.sqrt(128.0)
    index = lax.broadcasted_iota(jnp.int32, (CHUNK, ROWS), 0)
    for part in range(rows // ROWS):
        chunk_low, chunk_high, low, high = chunk_range(
            me * rows + part * ROWS, window_first, docs_ref
        )
        range_ref[2 * part] = chunk_low
        range_ref[2 * part + 1] = chunk_high
        low = low - window_first
        high = high - window_first
        peak_ref[...] = jnp.full_like(peak_ref, NEGATIVE)
        sum_ref[...] = jnp.zeros_like(sum_ref)

        def score_step(chunk, _):
            keys = window_ref[at_block(chunk, CHUNK), :]
            scores = nt_dot(keys, queries_ref[part])
            place = index + chunk * CHUNK
            seen = (place >= low) & (place < high)
            for h in range(0, stack, ROWS):
                masked = jnp.where(seen, scores[:, h : h + ROWS], NEGATIVE)
                score_ref[chunk, :, h : h + ROWS] = masked
                peak_ref[:, h : h + ROWS] = fold(peak_ref[:, h : h + ROWS], masked, jnp.max)
            return 0

        lax.fori_loop(chunk_low, chunk_high, score_step, 0)
        peak = jnp.max(peak_ref[...], axis=0, keepdims=True)

        def exp_step(chunk, _):
            probs = jnp.exp2((score_ref[chunk] - peak) * power)
            score_ref[chunk] = probs
            sum_ref[...] = fold(sum_ref[...], probs, jnp.sum)
            return 0

        lax.fori_loop(chunk_low, chunk_high, exp_step, 0)
        inverse = 1.0 / jnp.sum(sum_ref[...], axis=0, keepdims=True)

        def value_step(chunk, _):
            probs = (score_ref[chunk] * inverse).astype(BF16)
            probs_ref[part, chunk] = probs
            total_ref[at_block(chunk, CHUNK), :] += jnp.dot(
                probs, grads_ref[part], preferred_element_type=F32
            )
            return 0

        lax.fori_loop(chunk_low, chunk_high, value_step, 0)
    give_out(core, total_ref, own_ref, mine_ref, give_ref, 1.0)


def scores_kernel(
    range_ref, queries_ref, grads_ref, probs_ref, keys_ref, value_ref,
    r1, r2, r3, s1, s2, s3,
    grad_q_ref, own_ref, mine_ref, give_ref,
    values_ref, product_ref, delta_ref, query_ref, total_ref,
):
    rows = value_ref.shape[0]
    stack = queries_ref.shape[1]
    core = lax.axis_index("fsdp")
    place_window(core, values_ref, value_ref[...], (r1[0], r2[0], r3[0]), (s1[0], s2[0], s3[0]))
    total_ref[...] = jnp.zeros_like(total_ref)
    scaling = 1.0 / math.sqrt(128.0)
    for part in range(rows // ROWS):
        chunk_low, chunk_high = range_ref[2 * part], range_ref[2 * part + 1]
        delta_ref[...] = jnp.zeros_like(delta_ref)
        query_ref[...] = jnp.zeros_like(query_ref)

        def delta_step(chunk, _):
            product = nt_dot(values_ref[at_block(chunk, CHUNK), :], grads_ref[part])
            product_ref[chunk] = product
            terms = product * probs_ref[part, chunk].astype(F32)
            delta_ref[...] = fold(delta_ref[...], terms, jnp.sum)
            return 0

        lax.fori_loop(chunk_low, chunk_high, delta_step, 0)
        delta = jnp.sum(delta_ref[...], axis=0, keepdims=True)

        def grad_step(chunk, _):
            at = at_block(chunk, CHUNK)
            grad = (probs_ref[part, chunk].astype(F32) * (product_ref[chunk] - delta)).astype(BF16)
            total_ref[at, :] += jnp.dot(grad, queries_ref[part], preferred_element_type=F32)
            query_ref[...] += tn_dot(keys_ref[at, :], grad)
            return 0

        lax.fori_loop(chunk_low, chunk_high, grad_step, 0)
        for h in range(0, stack, ROWS):
            grad_q_ref[part * ROWS : (part + 1) * ROWS, h : h + ROWS] = (
                (query_ref[:, h : h + ROWS] * scaling).T.astype(BF16)
            )
    give_out(core, total_ref, own_ref, mine_ref, give_ref, scaling)


def pack_kernel(half_ref, other_ref, mine_ref, got_ref, value_ref, *outs):
    value = (half_ref[...] + other_ref[...]).astype(BF16)
    value_ref[...] = value
    for k, out in enumerate(outs):
        out[0] = value
        out[1] = (mine_ref[k] + got_ref[k].astype(F32)).astype(BF16)


def sum_blocks(own, other, mine, others):
    total = own + other
    for a, b in zip(mine, others):
        total = total + (a.astype(F32) + b.astype(F32))
    return total


def value_kernel(x_ref, z0, z1, z2, z3, c0, c1, c2, c3, part_ref, weight_ref):
    me = lax.axis_index("dp")
    width = z0.shape[0]
    for k, (near, cross) in enumerate(((z0, c0), (z1, c1), (z2, c2), (z3, c3))):
        owner = me ^ (2 * k)
        weight_ref[pl.ds(pl.multiple_of(owner * width, width), width), :] = near[...]
        there = owner ^ 1
        weight_ref[pl.ds(pl.multiple_of(there * width, width), width), :] = cross[...]
    part_ref[...] = nt_dot(x_ref[...], weight_ref[...])


def weight_grad_kernel(x_ref, a_ref, b_ref, r1, r2, r3, s1, s2, s3, grad_ref, *outs):
    me = lax.axis_index("dp")
    grad = sum_blocks(
        a_ref[...], b_ref[...], (r1[1], r2[1], r3[1]), (s1[1], s2[1], s3[1])
    ).astype(BF16)
    grad_ref[...] = grad
    depth = x_ref.shape[1]
    width = outs[0].shape[0]
    step = 512
    scratch = outs[8]
    for at in range(0, depth, step):
        scratch[:, at : at + step] = tn_dot(grad, x_ref[:, at : at + step])
    for k in range(4):
        owner = me ^ (2 * k)
        outs[k][...] = scratch[pl.ds(pl.multiple_of(owner * width, width), width), :]
        there = owner ^ 1
        rows = scratch[pl.ds(pl.multiple_of(there * width, width), width), :]
        outs[4 + k][...] = rows.astype(BF16)


def call(kernel, outs, scratch, limit_mib, smem, *args):
    return pl.pallas_call(
        kernel,
        in_specs=[SMEM] * smem + [VMEM] * (len(args) - smem),
        out_specs=[SMEM if len(shape) == 1 else VMEM for shape, _ in outs],
        out_shape=[jax.ShapeDtypeStruct(shape, kind) for shape, kind in outs],
        scratch_shapes=scratch,
        compiler_params=pltpu.CompilerParams(vmem_limit_bytes=limit_mib << 20),
        cost_estimate=pl.CostEstimate(flops=1 << 30, bytes_accessed=4 << 20, transcendentals=0),
    )(*args)


def body(layer_input, w_value, queries, keys, grad_out, doc_lengths, prefix_spans):
    rows, depth = layer_input.shape
    head = keys.shape[1]
    heads = queries.shape[1] // head
    dp = lax.axis_size("dp")
    window = (2 * SPAN + 1) * rows
    chunks = window // CHUNK
    parts = rows // ROWS
    stack = heads * ROWS
    weight = w_value.T
    width = weight.shape[0]
    direct = dp == 8
    steps = range(SPAN)

    docs = jnp.concatenate([doc_lengths, prefix_spans])
    query_stack = stack_heads(queries, head)
    grad_stack = stack_heads(grad_out, head)
    mine = [fan_out(keys, k) for k in steps]
    other = [core_swap(after(block, docs, query_stack, grad_stack)) for block in mine]
    if direct:
        weight = after(weight, mine[0])
        z3, z2, z1 = (dp_swap(weight, 2 * k) for k in (3, 2, 1))
        cross0 = dp_swap(weight, 1)

    ranges, probs, key_window, own_v, mine_v, give_v = call(
        weights_kernel,
        [
            ((2 * parts,), jnp.int32),
            ((parts, chunks, CHUNK, stack), BF16),
            ((window, head), BF16),
            ((rows, head), F32),
            ((SPAN, rows, head), F32),
            ((SPAN, rows, head), BF16),
        ],
        [
            pltpu.VMEM((chunks, CHUNK, stack), F32),
            pltpu.VMEM((8, stack), F32),
            pltpu.VMEM((8, stack), F32),
            pltpu.VMEM((window, head), F32),
        ],
        20, 1,
        docs, query_stack, grad_stack, keys, *mine, *other,
    )
    got_v = core_swap(give_v)
    other_v = core_swap(own_v)

    if direct:
        cross = [cross0] + [dp_swap(block, 1) for block in (z1, z2, z3)]
        value_part, full_weight = call(
            value_kernel,
            [((rows, head), F32), ((head, depth), BF16)],
            [], 12, 0,
            layer_input, weight, z1, z2, z3, *cross,
        )
    else:
        full_weight = lax.all_gather(weight, "dp", axis=0, tiled=True)
        value_part = nt_dot(layer_input, full_weight)
    value, *packs = call(
        pack_kernel,
        [((rows, head), BF16)] + [((2, rows, head), BF16)] * SPAN,
        [], 8, 0,
        value_part, core_swap(value_part), mine_v, got_v,
    )
    mine = [fan_out(pack, k) for pack, k in zip(packs, steps)]
    other = [core_swap(block) for block in mine]

    if direct:
        grad_value, *blocks = call(
            weight_grad_kernel,
            [((rows, head), BF16)] + [((width, depth), F32)] * 4 + [((width, depth), BF16)] * 4,
            [pltpu.VMEM((head, depth), F32)], 16, 0,
            layer_input, own_v, other_v, *mine, *other,
        )
        keep, send = blocks[:4], blocks[4:]
        total = keep[0]
        for k in (3, 2, 1):
            pair = (keep[k] + dp_swap(send[k], 1).astype(F32)).astype(BF16)
            total = total + dp_swap(pair, 2 * k).astype(F32)
        total = total + dp_swap(send[0], 1).astype(F32)
        grad_weight = total.T
    else:
        grad_value = sum_blocks(
            own_v, other_v, [block[1] for block in mine], [block[1] for block in other]
        ).astype(BF16)
        grad_weight = lax.psum_scatter(
            tn_dot(grad_value, layer_input), "dp", scatter_dimension=0, tiled=True
        ).T
    grad_queries, own_k, mine_k, give_k = call(
        scores_kernel,
        [
            ((rows, heads * head), BF16),
            ((rows, head), F32),
            ((SPAN, rows, head), F32),
            ((SPAN, rows, head), BF16),
        ],
        [
            pltpu.VMEM((window, head), BF16),
            pltpu.VMEM((chunks, CHUNK, stack), F32),
            pltpu.VMEM((8, stack), F32),
            pltpu.VMEM((head, stack), F32),
            pltpu.VMEM((window, head), F32),
        ],
        20, 1,
        after(ranges, grad_value), query_stack, grad_stack, probs, key_window, value, *mine, *other,
    )
    got_k = core_swap(give_k)
    mine = [
        fan_out((mine_k[k] + got_k[k].astype(F32)).astype(BF16), k) for k in steps
    ]
    other = [core_swap(block) for block in mine]
    grad_input = jnp.dot(
        grad_value, full_weight, preferred_element_type=F32
    ).astype(BF16)
    grad_keys = sum_blocks(own_k, core_swap(own_k), mine, other).astype(BF16)
    return (grad_input, grad_queries, grad_keys, grad_weight)


def solution(mesh):
    in_specs = (
        P(("groups", "dp"), "fsdp"),
        P("fsdp", "dp"),
        P(("groups", "dp"), "fsdp"),
        P(("groups", "dp"), None),
        P(("groups", "dp"), "fsdp"),
        P("groups"),
        P("groups"),
    )
    out_specs = (
        P(("groups", "dp"), "fsdp"),
        P(("groups", "dp"), "fsdp"),
        P(("groups", "dp"), None),
        P(("groups", "fsdp"), "dp"),
    )
    return jax.shard_map(body, mesh=mesh, in_specs=in_specs, out_specs=out_specs, check_vma=False)
```

```python
import math

import jax
import jax.numpy as jnp
from jax import lax
from jax.experimental import pallas as pl
from jax.experimental.pallas import tpu as pltpu
from jax.sharding import PartitionSpec as P

SPAN = 3
NEGATIVE = -1e30
CHUNK = 256
ROWS = 128
BOTH = ("dp", "fsdp")
F32 = jnp.float32
BF16 = jnp.bfloat16
VMEM = pl.BlockSpec(memory_space=pltpu.VMEM)
SMEM = pl.BlockSpec(memory_space=pltpu.SMEM)
HBM = pl.BlockSpec(memory_space=pl.ANY)


def core_swap(value):
    return lax.ppermute(value, "fsdp", [(0, 1), (1, 0)])


def dp_swap(value, mask):
    count = lax.axis_size("dp")
    return lax.ppermute(value, "dp", [(i, i ^ mask) for i in range(count)])


def reach(step, core, odd):
    turn = 1 - 2 * odd
    return ((-3 * turn, turn - 2), (-2, turn + 2), (2, turn))[step][core]


def offset(step, core, odd, sign):
    turn = 1 - 2 * odd
    near = ((0, -2), (-2, 2), (2, 0))[step]
    first = -3 * turn if step == 0 else sign * near[0]
    return jnp.where(core == 0, first, sign * near[1] + turn)


def fan_out(value, step):
    count = lax.axis_size("dp")
    pairs = [(2 * i + c, 2 * (i + reach(step, c, i % 2)) + c) for i in range(count) for c in (0, 1)]
    return lax.ppermute(value, BOTH, [(i, j) for i, j in pairs if 0 <= j < 2 * count])


def after(value, *others):
    return lax.optimization_barrier((value, *others))[0]


def chunk_range(first, window_first, docs_ref):
    last = first + ROWS - 1
    zero = jnp.int32(0)
    count = docs_ref.shape[0] // 2
    position = first + lax.broadcasted_iota(jnp.int32, (1, ROWS), 1)
    low, high = jnp.zeros((1, ROWS), jnp.int32), jnp.zeros((1, ROWS), jnp.int32)

    def step(doc, carry):
        start, least, most, low, high = carry
        length = docs_ref[doc]
        end = start + length
        bound = start + jnp.minimum(docs_ref[count + doc], length)
        least = jnp.where((start <= first) & (first < end), start, least)
        most = jnp.where((start <= last) & (last < end), jnp.maximum(last + 1, bound), most)
        inside = (position >= start) & (position < end)
        low = jnp.where(inside, start, low)
        high = jnp.where(inside, jnp.maximum(position + 1, bound), high)
        return (end, least, most, low, high)

    carry = (zero, zero, zero, low, high)
    if count <= 8:
        for doc in range(count):
            carry = step(doc, carry)
    else:
        carry = lax.fori_loop(0, count, step, carry)
    _, least, most, low, high = carry
    chunk_low = lax.div(least - window_first, CHUNK)
    chunk_high = lax.div(most - window_first + CHUNK - 1, CHUNK)
    return chunk_low, chunk_high, low, high


def at_block(index, rows):
    return pl.ds(pl.multiple_of(index * rows, rows), rows)


def place_window(core, window_ref, own, mine, other):
    rows = own.shape[0]
    odd = lax.rem(lax.axis_index("dp"), 2)
    window_ref[SPAN * rows : (SPAN + 1) * rows, :] = own
    for k in range(SPAN):
        window_ref[at_block(SPAN + offset(k, core, odd, -1), rows), :] = mine[k]
        window_ref[at_block(SPAN + offset(k, 1 - core, odd, -1), rows), :] = other[k]


def give_out(core, total_ref, own_ref, mine_ref, give_ref, factor):
    rows = own_ref.shape[0]
    odd = lax.rem(lax.axis_index("dp"), 2)
    own_ref[...] = total_ref[SPAN * rows : (SPAN + 1) * rows, :] * factor
    for k in range(SPAN):
        mine_ref[k] = total_ref[at_block(SPAN + offset(k, core, odd, 1), rows), :] * factor
        there = total_ref[at_block(SPAN + offset(k, 1 - core, odd, 1), rows), :] * factor
        give_ref[k] = there.astype(BF16)


def stack_heads(value, head):
    rows, wide = value.shape
    split = value.reshape(rows // ROWS, ROWS, wide // head, head)
    return split.transpose(0, 2, 1, 3).reshape(rows // ROWS, -1, head)


def nt_dot(a, b):
    return lax.dot_general(a, b, (((1,), (1,)), ((), ())), preferred_element_type=F32)


def tn_dot(a, b):
    return lax.dot_general(a, b, (((0,), (0,)), ((), ())), preferred_element_type=F32)


def fold(total, value, reduce):
    rows, lanes = value.shape
    return reduce(jnp.concatenate([total[None], value.reshape(rows // 8, 8, lanes)]), axis=0)


def limits_kernel(docs_ref, info_ref):
    rows = info_ref.shape[0] * ROWS
    first = lax.axis_index("dp") * rows
    window_first = first - SPAN * rows
    info_ref[...] = jnp.zeros_like(info_ref)
    for part in range(rows // ROWS):
        chunk_low, chunk_high, low, high = chunk_range(
            first + part * ROWS, window_first, docs_ref
        )
        info_ref[part, 0:1] = low - window_first
        info_ref[part, 1:2] = high - window_first
        info_ref[part, 2:3] = jnp.zeros_like(low) + chunk_low
        info_ref[part, 3:4] = jnp.zeros_like(low) + (chunk_high - chunk_low)


def by_count(count, most, body):
    for n in range(1, most + 1):

        @pl.when(count == n)
        def _():
            body(n)


def weights_kernel(
    info_ref, queries_ref, grads_ref, key_ref, r1, r2, r3, s1, s2, s3,
    probs_ref, window_ref, own_ref, mine_ref, give_ref,
    score_ref, total_ref,
):
    rows = key_ref.shape[0]
    stack = queries_ref.shape[1]
    core = lax.axis_index("fsdp")
    place_window(
        core, window_ref, key_ref[...], (r1[...], r2[...], r3[...]), (s1[...], s2[...], s3[...])
    )
    total_ref[...] = jnp.zeros_like(total_ref)
    power = math.log2(math.e) / math.sqrt(128.0)
    index = lax.broadcasted_iota(jnp.int32, (CHUNK, ROWS), 0)

    def part_step(part):
        chunk_low = info_ref[part, 2:3][0, 0]
        low = info_ref[part, 0:1] - chunk_low * CHUNK
        high = info_ref[part, 1:2] - chunk_low * CHUNK

        def chunks(count):
            peak = jnp.full((8, stack), NEGATIVE, F32)
            for i in range(count):
                scores = nt_dot(window_ref[at_block(chunk_low + i, CHUNK), :], queries_ref[part])
                place = index + i * CHUNK
                seen = (place >= low) & (place < high)
                seen = jnp.concatenate([seen] * (stack // ROWS), axis=1)
                masked = jnp.where(seen, scores, NEGATIVE)
                score_ref[i] = masked
                peak = fold(peak, masked, jnp.max)
            peak = jnp.max(peak, axis=0, keepdims=True)
            total = jnp.zeros((8, stack), F32)
            for i in range(count):
                probs = jnp.exp2((score_ref[i] - peak) * power)
                score_ref[i] = probs
                total = fold(total, probs, jnp.sum)
            inverse = 1.0 / jnp.sum(total, axis=0, keepdims=True)
            for i in range(count):
                probs = (score_ref[i] * inverse).astype(BF16)
                probs_ref[part, i] = probs
                total_ref[at_block(chunk_low + i, CHUNK), :] += jnp.dot(
                    probs, grads_ref[part], preferred_element_type=F32
                )

        by_count(info_ref[part, 3:4][0, 0], probs_ref.shape[1], chunks)

    for part in range(rows // ROWS):
        part_step(part)
    give_out(core, total_ref, own_ref, mine_ref, give_ref, 1.0)


def scores_kernel(
    info_ref, queries_ref, grads_ref, probs_ref, keys_ref, value_ref,
    r1, r2, r3, s1, s2, s3,
    query_ref, own_ref, mine_ref, give_ref,
    values_ref, product_ref, total_ref,
):
    rows = value_ref.shape[0]
    stack = queries_ref.shape[1]
    core = lax.axis_index("fsdp")
    place_window(core, values_ref, value_ref[...], (r1[0], r2[0], r3[0]), (s1[0], s2[0], s3[0]))
    total_ref[...] = jnp.zeros_like(total_ref)
    scaling = 1.0 / math.sqrt(128.0)

    def part_step(part, _):
        chunk_low = info_ref[part, 2:3][0, 0]

        def chunks(count):
            delta = jnp.zeros((8, stack), F32)
            for i in range(count):
                product = nt_dot(values_ref[at_block(chunk_low + i, CHUNK), :], grads_ref[part])
                product_ref[i] = product
                delta = fold(delta, product * probs_ref[part, i].astype(F32), jnp.sum)
            delta = jnp.sum(delta, axis=0, keepdims=True)
            query = jnp.zeros(query_ref.shape[1:], F32)
            for i in range(count):
                at = at_block(chunk_low + i, CHUNK)
                grad = (probs_ref[part, i].astype(F32) * (product_ref[i] - delta)).astype(BF16)
                total_ref[at, :] += jnp.dot(grad, queries_ref[part], preferred_element_type=F32)
                query += tn_dot(keys_ref[at, :], grad)
            query_ref[part] = query * scaling

        by_count(info_ref[part, 3:4][0, 0], probs_ref.shape[1], chunks)
        return 0

    lax.fori_loop(0, rows // ROWS, part_step, 0)
    give_out(core, total_ref, own_ref, mine_ref, give_ref, scaling)


def pack_kernel(half_ref, other_ref, mine_ref, got_ref, value_ref, *outs):
    value = (half_ref[...] + other_ref[...]).astype(BF16)
    value_ref[...] = value
    for k, out in enumerate(outs):
        out[0] = value
        out[1] = (mine_ref[k] + got_ref[k].astype(F32)).astype(BF16)


def sum_blocks(own, other, mine, others):
    total = own + other
    for a, b in zip(mine, others):
        total = total + (a.astype(F32) + b.astype(F32))
    return total


def value_kernel(x_ref, z0, z1, z2, z3, c0, c1, c2, c3, part_ref, weight_ref):
    me = lax.axis_index("dp")
    width = z0.shape[0]
    for k, (near, cross) in enumerate(((z0, c0), (z1, c1), (z2, c2), (z3, c3))):
        owner = me ^ (2 * k)
        weight_ref[pl.ds(pl.multiple_of(owner * width, width), width), :] = near[...]
        there = owner ^ 1
        weight_ref[pl.ds(pl.multiple_of(there * width, width), width), :] = cross[...]
    part_ref[...] = nt_dot(x_ref[...], weight_ref[...])


def weight_grad_kernel(x_ref, a_ref, b_ref, r1, r2, r3, s1, s2, s3, grad_ref, *outs):
    me = lax.axis_index("dp")
    grad = sum_blocks(
        a_ref[...], b_ref[...], (r1[1], r2[1], r3[1]), (s1[1], s2[1], s3[1])
    ).astype(BF16)
    grad_ref[...] = grad
    depth = x_ref.shape[1]
    width = outs[0].shape[0]
    step = 512
    scratch = outs[8]
    for at in range(0, depth, step):
        scratch[:, at : at + step] = tn_dot(grad, x_ref[:, at : at + step])
    for k in range(4):
        owner = me ^ (2 * k)
        outs[k][...] = scratch[pl.ds(pl.multiple_of(owner * width, width), width), :]
        there = owner ^ 1
        rows = scratch[pl.ds(pl.multiple_of(there * width, width), width), :]
        outs[4 + k][...] = rows.astype(BF16)


def finish_kernel(grad_ref, weight_ref, query_ref, out_hbm, query_hbm, out_ref, turned_ref, sems):
    copies = []
    for part in range(query_ref.shape[0]):
        for h in range(0, query_ref.shape[2], ROWS):
            turned_ref[part * ROWS : (part + 1) * ROWS, h : h + ROWS] = (
                query_ref[part, :, h : h + ROWS].T.astype(BF16)
            )
    copies.append(pltpu.make_async_copy(turned_ref, query_hbm, sems.at[8]))
    copies[-1].start()
    step = out_ref.shape[1] // 8
    for i in range(8):
        cut = slice(i * step, (i + 1) * step)
        out_ref[:, cut] = jnp.dot(
            grad_ref[...], weight_ref[:, cut], preferred_element_type=F32
        ).astype(BF16)
        copies.append(
            pltpu.make_async_copy(out_ref.at[:, cut], out_hbm.at[:, cut], sems.at[i])
        )
        copies[-1].start()
    for copy in copies:
        copy.wait()


def call(kernel, outs, scratch, limit_mib, smem, *args):
    return pl.pallas_call(
        kernel,
        in_specs=[SMEM] * smem + [VMEM] * (len(args) - smem),
        out_specs=[HBM if kernel is finish_kernel else VMEM for _ in outs],
        out_shape=[jax.ShapeDtypeStruct(shape, kind) for shape, kind in outs],
        scratch_shapes=scratch,
        compiler_params=pltpu.CompilerParams(vmem_limit_bytes=limit_mib << 20),
        cost_estimate=pl.CostEstimate(flops=1 << 30, bytes_accessed=4 << 20, transcendentals=0),
    )(*args)


def body(layer_input, w_value, queries, keys, grad_out, doc_lengths, prefix_spans):
    rows, depth = layer_input.shape
    head = keys.shape[1]
    heads = queries.shape[1] // head
    dp = lax.axis_size("dp")
    window = (2 * SPAN + 1) * rows
    chunks = window // CHUNK
    parts = rows // ROWS
    stack = heads * ROWS
    weight = w_value.T
    width = weight.shape[0]
    direct = dp == 8
    steps = range(SPAN)

    (info,) = call(
        limits_kernel,
        [((parts, 8, ROWS), jnp.int32)],
        [], 4, 1,
        jnp.concatenate([doc_lengths, prefix_spans]),
    )
    query_stack = stack_heads(queries, head)
    grad_stack = stack_heads(grad_out, head)
    mine = [fan_out(keys, k) for k in steps]
    other = [core_swap(after(block, info, query_stack, grad_stack)) for block in mine]
    if direct:
        weight = after(weight, mine[0])
        z3, z2, z1 = (dp_swap(weight, 2 * k) for k in (3, 2, 1))
        cross0 = dp_swap(weight, 1)

    probs, key_window, own_v, mine_v, give_v = call(
        weights_kernel,
        [
            ((parts, chunks, CHUNK, stack), BF16),
            ((window, head), BF16),
            ((rows, head), F32),
            ((SPAN, rows, head), F32),
            ((SPAN, rows, head), BF16),
        ],
        [
            pltpu.VMEM((chunks, CHUNK, stack), F32),
            pltpu.VMEM((window, head), F32),
        ],
        20, 0,
        info, query_stack, grad_stack, keys, *mine, *other,
    )
    got_v = core_swap(give_v)
    other_v = core_swap(own_v)

    if direct:
        cross = [cross0] + [dp_swap(block, 1) for block in (z1, z2, z3)]
        value_part, full_weight = call(
            value_kernel,
            [((rows, head), F32), ((head, depth), BF16)],
            [], 12, 0,
            layer_input, weight, z1, z2, z3, *cross,
        )
    else:
        full_weight = lax.all_gather(weight, "dp", axis=0, tiled=True)
        value_part = nt_dot(layer_input, full_weight)
    value, *packs = call(
        pack_kernel,
        [((rows, head), BF16)] + [((2, rows, head), BF16)] * SPAN,
        [], 8, 0,
        value_part, core_swap(value_part), mine_v, got_v,
    )
    mine = [fan_out(pack, k) for pack, k in zip(packs, steps)]
    other = [core_swap(block) for block in mine]

    if direct:
        grad_value, *blocks = call(
            weight_grad_kernel,
            [((rows, head), BF16)] + [((width, depth), F32)] * 4 + [((width, depth), BF16)] * 4,
            [pltpu.VMEM((head, depth), F32)], 16, 0,
            layer_input, own_v, other_v, *mine, *other,
        )
        keep, send = blocks[:4], blocks[4:]
        total = keep[0]
        for k in (3, 2, 1):
            pair = (keep[k] + dp_swap(send[k], 1).astype(F32)).astype(BF16)
            total = total + dp_swap(pair, 2 * k).astype(F32)
        total = total + dp_swap(send[0], 1).astype(F32)
        grad_weight = total.T
    else:
        grad_value = sum_blocks(
            own_v, other_v, [block[1] for block in mine], [block[1] for block in other]
        ).astype(BF16)
        grad_weight = lax.psum_scatter(
            tn_dot(grad_value, layer_input), "dp", scatter_dimension=0, tiled=True
        ).T
    grad_stack_q, own_k, mine_k, give_k = call(
        scores_kernel,
        [
            ((parts, head, stack), F32),
            ((rows, head), F32),
            ((SPAN, rows, head), F32),
            ((SPAN, rows, head), BF16),
        ],
        [
            pltpu.VMEM((window, head), BF16),
            pltpu.VMEM((chunks, CHUNK, stack), F32),
            pltpu.VMEM((window, head), F32),
        ],
        20, 0,
        after(info, grad_value), query_stack, grad_stack, probs, key_window, value, *mine, *other,
    )
    got_k = core_swap(give_k)
    mine = [
        fan_out((mine_k[k] + got_k[k].astype(F32)).astype(BF16), k) for k in steps
    ]
    other = [core_swap(block) for block in mine]
    grad_input, grad_queries = call(
        finish_kernel,
        [((rows, depth), BF16), ((rows, heads * head), BF16)],
        [
            pltpu.VMEM((rows, depth), BF16),
            pltpu.VMEM((rows, heads * head), BF16),
            pltpu.SemaphoreType.DMA((9,)),
        ],
        12, 0,
        grad_value, full_weight, grad_stack_q,
    )
    grad_keys = sum_blocks(own_k, core_swap(own_k), mine, other).astype(BF16)
    return (grad_input, grad_queries, grad_keys, grad_weight)


def solution(mesh):
    in_specs = (
        P(("groups", "dp"), "fsdp"),
        P("fsdp", "dp"),
        P(("groups", "dp"), "fsdp"),
        P(("groups", "dp"), None),
        P(("groups", "dp"), "fsdp"),
        P("groups"),
        P("groups"),
    )
    out_specs = (
        P(("groups", "dp"), "fsdp"),
        P(("groups", "dp"), "fsdp"),
        P(("groups", "dp"), None),
        P(("groups", "fsdp"), "dp"),
    )
    return jax.shard_map(body, mesh=mesh, in_specs=in_specs, out_specs=out_specs, check_vma=False)
```

```python
import math

import jax
import jax.numpy as jnp
from jax import lax
from jax.experimental import pallas as pl
from jax.experimental.pallas import tpu as pltpu
from jax.sharding import PartitionSpec as P

SPAN = 3
NEGATIVE = -1e30
CHUNK = 256
ROWS = 128
BOTH = ("dp", "fsdp")
F32 = jnp.float32
BF16 = jnp.bfloat16
VMEM = pl.BlockSpec(memory_space=pltpu.VMEM)
SMEM = pl.BlockSpec(memory_space=pltpu.SMEM)
HBM = pl.BlockSpec(memory_space=pl.ANY)


def core_swap(value):
    return lax.ppermute(value, "fsdp", [(0, 1), (1, 0)])


def dp_swap(value, mask):
    count = lax.axis_size("dp")
    return lax.ppermute(value, "dp", [(i, i ^ mask) for i in range(count)])


def reach(step, core, odd):
    turn = 1 - 2 * odd
    return ((-3 * turn, turn - 2), (-2, turn + 2), (2, turn))[step][core]


def offset(step, core, odd, sign):
    turn = 1 - 2 * odd
    near = ((0, -2), (-2, 2), (2, 0))[step]
    first = -3 * turn if step == 0 else sign * near[0]
    return jnp.where(core == 0, first, sign * near[1] + turn)


def fan_out(value, step):
    count = lax.axis_size("dp")
    pairs = [(2 * i + c, 2 * (i + reach(step, c, i % 2)) + c) for i in range(count) for c in (0, 1)]
    return lax.ppermute(value, BOTH, [(i, j) for i, j in pairs if 0 <= j < 2 * count])


def after(value, *others):
    return lax.optimization_barrier((value, *others))[0]


def chunk_range(first, window_first, docs_ref):
    last = first + ROWS - 1
    zero = jnp.int32(0)
    count = docs_ref.shape[0] // 2
    position = first + lax.broadcasted_iota(jnp.int32, (1, ROWS), 1)
    low, high = jnp.zeros((1, ROWS), jnp.int32), jnp.zeros((1, ROWS), jnp.int32)

    def step(doc, carry):
        start, least, most, low, high = carry
        length = docs_ref[doc]
        end = start + length
        bound = start + jnp.minimum(docs_ref[count + doc], length)
        least = jnp.where((start <= first) & (first < end), start, least)
        most = jnp.where((start <= last) & (last < end), jnp.maximum(last + 1, bound), most)
        inside = (position >= start) & (position < end)
        low = jnp.where(inside, start, low)
        high = jnp.where(inside, jnp.maximum(position + 1, bound), high)
        return (end, least, most, low, high)

    carry = (zero, zero, zero, low, high)
    if count <= 8:
        for doc in range(count):
            carry = step(doc, carry)
    else:
        carry = lax.fori_loop(0, count, step, carry)
    _, least, most, low, high = carry
    chunk_low = lax.div(least - window_first, CHUNK)
    chunk_high = lax.div(most - window_first + CHUNK - 1, CHUNK)
    return chunk_low, chunk_high, low, high


def at_block(index, rows):
    return pl.ds(pl.multiple_of(index * rows, rows), rows)


def place_window(core, window_ref, own, mine, other):
    rows = own.shape[0]
    odd = lax.rem(lax.axis_index("dp"), 2)
    window_ref[SPAN * rows : (SPAN + 1) * rows, :] = own
    for k in range(SPAN):
        window_ref[at_block(SPAN + offset(k, core, odd, -1), rows), :] = mine[k]
        window_ref[at_block(SPAN + offset(k, 1 - core, odd, -1), rows), :] = other[k]


def give_out(core, total_ref, own_ref, mine_ref, give_ref, factor):
    rows = own_ref.shape[0]
    odd = lax.rem(lax.axis_index("dp"), 2)
    own_ref[...] = total_ref[SPAN * rows : (SPAN + 1) * rows, :] * factor
    for k in range(SPAN):
        mine_ref[k] = total_ref[at_block(SPAN + offset(k, core, odd, 1), rows), :] * factor
        there = total_ref[at_block(SPAN + offset(k, 1 - core, odd, 1), rows), :] * factor
        give_ref[k] = there.astype(BF16)


def stack_heads(value, head):
    rows, wide = value.shape
    split = value.reshape(rows // ROWS, ROWS, wide // head, head)
    return split.transpose(0, 2, 1, 3).reshape(rows // ROWS, -1, head)


def nt_dot(a, b):
    return lax.dot_general(a, b, (((1,), (1,)), ((), ())), preferred_element_type=F32)


def tn_dot(a, b):
    return lax.dot_general(a, b, (((0,), (0,)), ((), ())), preferred_element_type=F32)


def fold(total, value, reduce):
    rows, lanes = value.shape
    return reduce(jnp.concatenate([total[None], value.reshape(rows // 8, 8, lanes)]), axis=0)


def limits_kernel(docs_ref, info_ref):
    rows = info_ref.shape[0] * ROWS
    first = lax.axis_index("dp") * rows
    window_first = first - SPAN * rows
    info_ref[...] = jnp.zeros_like(info_ref)
    for part in range(rows // ROWS):
        chunk_low, chunk_high, low, high = chunk_range(
            first + part * ROWS, window_first, docs_ref
        )
        info_ref[part, 0:1] = low - window_first
        info_ref[part, 1:2] = high - window_first
        info_ref[part, 2:3] = jnp.zeros_like(low) + chunk_low
        info_ref[part, 3:4] = jnp.zeros_like(low) + (chunk_high - chunk_low)


def by_count(count, most, body):
    for n in range(1, most + 1):

        @pl.when(count == n)
        def _():
            body(n)


def weights_kernel(
    info_ref, queries_ref, grads_ref, key_ref, r1, r2, r3, s1, s2, s3,
    probs_ref, window_ref, own_ref, mine_ref, give_ref,
    score_ref, total_ref,
):
    rows = key_ref.shape[0]
    stack = queries_ref.shape[1]
    core = lax.axis_index("fsdp")
    place_window(
        core, window_ref, key_ref[...], (r1[...], r2[...], r3[...]), (s1[...], s2[...], s3[...])
    )
    total_ref[...] = jnp.zeros_like(total_ref)
    power = math.log2(math.e) / math.sqrt(128.0)
    index = lax.broadcasted_iota(jnp.int32, (CHUNK, ROWS), 0)

    def part_step(part):
        chunk_low = info_ref[part, 2:3][0, 0]
        low = info_ref[part, 0:1] - chunk_low * CHUNK
        high = info_ref[part, 1:2] - chunk_low * CHUNK

        def chunks(count):
            peak = jnp.full((8, stack), NEGATIVE, F32)
            for i in range(count):
                scores = nt_dot(window_ref[at_block(chunk_low + i, CHUNK), :], queries_ref[part])
                place = index + i * CHUNK
                seen = (place >= low) & (place < high)
                seen = jnp.concatenate([seen] * (stack // ROWS), axis=1)
                masked = jnp.where(seen, scores, NEGATIVE)
                score_ref[i] = masked
                peak = fold(peak, masked, jnp.max)
            peak = jnp.max(peak, axis=0, keepdims=True)
            total = jnp.zeros((8, stack), F32)
            for i in range(count):
                probs = jnp.exp2((score_ref[i] - peak) * power)
                score_ref[i] = probs
                total = fold(total, probs, jnp.sum)
            inverse = 1.0 / jnp.sum(total, axis=0, keepdims=True)
            for i in range(count):
                probs = (score_ref[i] * inverse).astype(BF16)
                probs_ref[part, i] = probs
                total_ref[at_block(chunk_low + i, CHUNK), :] += jnp.dot(
                    probs, grads_ref[part], preferred_element_type=F32
                )

        by_count(info_ref[part, 3:4][0, 0], probs_ref.shape[1], chunks)

    for part in range(rows // ROWS):
        part_step(part)
    give_out(core, total_ref, own_ref, mine_ref, give_ref, 1.0)


def scores_kernel(
    info_ref, queries_ref, grads_ref, probs_ref, keys_ref, value_ref,
    r1, r2, r3, s1, s2, s3,
    query_ref, own_ref, mine_ref, give_ref,
    values_ref, product_ref, total_ref,
):
    rows = value_ref.shape[0]
    stack = queries_ref.shape[1]
    core = lax.axis_index("fsdp")
    place_window(core, values_ref, value_ref[...], (r1[0], r2[0], r3[0]), (s1[0], s2[0], s3[0]))
    total_ref[...] = jnp.zeros_like(total_ref)
    scaling = 1.0 / math.sqrt(128.0)

    def part_step(part, _):
        chunk_low = info_ref[part, 2:3][0, 0]

        def chunks(count):
            delta = jnp.zeros((8, stack), F32)
            for i in range(count):
                product = nt_dot(values_ref[at_block(chunk_low + i, CHUNK), :], grads_ref[part])
                product_ref[i] = product
                delta = fold(delta, product * probs_ref[part, i].astype(F32), jnp.sum)
            delta = jnp.sum(delta, axis=0, keepdims=True)
            query = jnp.zeros(query_ref.shape[1:], F32)
            for i in range(count):
                at = at_block(chunk_low + i, CHUNK)
                grad = (probs_ref[part, i].astype(F32) * (product_ref[i] - delta)).astype(BF16)
                total_ref[at, :] += jnp.dot(grad, queries_ref[part], preferred_element_type=F32)
                query += tn_dot(keys_ref[at, :], grad)
            query_ref[part] = query * scaling

        by_count(info_ref[part, 3:4][0, 0], probs_ref.shape[1], chunks)
        return 0

    lax.fori_loop(0, rows // ROWS, part_step, 0)
    give_out(core, total_ref, own_ref, mine_ref, give_ref, scaling)


def pack_kernel(half_ref, other_ref, mine_ref, got_ref, value_ref, *outs):
    value = (half_ref[...] + other_ref[...]).astype(BF16)
    value_ref[...] = value
    for k, out in enumerate(outs):
        out[0] = value
        out[1] = (mine_ref[k] + got_ref[k].astype(F32)).astype(BF16)


def sum_blocks(own, other, mine, others):
    total = own + other
    for a, b in zip(mine, others):
        total = total + (a.astype(F32) + b.astype(F32))
    return total


def value_kernel(x_ref, z0, z1, z2, z3, c0, c1, c2, c3, part_ref, weight_ref):
    me = lax.axis_index("dp")
    width = z0.shape[0]
    for k, (near, cross) in enumerate(((z0, c0), (z1, c1), (z2, c2), (z3, c3))):
        owner = me ^ (2 * k)
        weight_ref[pl.ds(pl.multiple_of(owner * width, width), width), :] = near[...]
        there = owner ^ 1
        weight_ref[pl.ds(pl.multiple_of(there * width, width), width), :] = cross[...]
    part_ref[...] = nt_dot(x_ref[...], weight_ref[...])


def weight_grad_kernel(x_ref, a_ref, b_ref, r1, r2, r3, s1, s2, s3, grad_ref, *outs):
    me = lax.axis_index("dp")
    grad = sum_blocks(
        a_ref[...], b_ref[...], (r1[1], r2[1], r3[1]), (s1[1], s2[1], s3[1])
    ).astype(BF16)
    grad_ref[...] = grad
    depth = x_ref.shape[1]
    width = outs[0].shape[0]
    step = 512
    scratch = outs[8]
    for at in range(0, depth, step):
        scratch[:, at : at + step] = tn_dot(grad, x_ref[:, at : at + step])
    for k in range(4):
        owner = me ^ (2 * k)
        outs[k][...] = scratch[pl.ds(pl.multiple_of(owner * width, width), width), :]
        there = owner ^ 1
        rows = scratch[pl.ds(pl.multiple_of(there * width, width), width), :]
        outs[4 + k][...] = rows.astype(BF16)


def finish_kernel(grad_ref, weight_ref, query_ref, out_hbm, query_hbm, out_ref, turned_ref, sems):
    copies = []
    for part in range(query_ref.shape[0]):
        for h in range(0, query_ref.shape[2], ROWS):
            turned_ref[part * ROWS : (part + 1) * ROWS, h : h + ROWS] = (
                query_ref[part, :, h : h + ROWS].T.astype(BF16)
            )
    copies.append(pltpu.make_async_copy(turned_ref, query_hbm, sems.at[8]))
    copies[-1].start()
    step = out_ref.shape[1] // 8
    for i in range(8):
        cut = slice(i * step, (i + 1) * step)
        out_ref[:, cut] = jnp.dot(
            grad_ref[...], weight_ref[:, cut], preferred_element_type=F32
        ).astype(BF16)
        copies.append(
            pltpu.make_async_copy(out_ref.at[:, cut], out_hbm.at[:, cut], sems.at[i])
        )
        copies[-1].start()
    for copy in copies:
        copy.wait()


def call(kernel, outs, scratch, limit_mib, smem, *args):
    return pl.pallas_call(
        kernel,
        in_specs=[SMEM] * smem + [VMEM] * (len(args) - smem),
        out_specs=[HBM if kernel is finish_kernel else VMEM for _ in outs],
        out_shape=[jax.ShapeDtypeStruct(shape, kind) for shape, kind in outs],
        scratch_shapes=scratch,
        compiler_params=pltpu.CompilerParams(vmem_limit_bytes=limit_mib << 20),
        cost_estimate=pl.CostEstimate(flops=1 << 30, bytes_accessed=4 << 20, transcendentals=0),
    )(*args)


def body(layer_input, w_value, queries, keys, grad_out, doc_lengths, prefix_spans):
    rows, depth = layer_input.shape
    head = keys.shape[1]
    heads = queries.shape[1] // head
    dp = lax.axis_size("dp")
    window = (2 * SPAN + 1) * rows
    chunks = window // CHUNK
    parts = rows // ROWS
    stack = heads * ROWS
    weight = w_value.T
    width = weight.shape[0]
    direct = dp == 8
    steps = range(SPAN)

    docs = jnp.concatenate([doc_lengths, prefix_spans])
    if direct:
        z3, z2, z1 = (dp_swap(weight, 2 * k) for k in (3, 2, 1))
        cross0 = dp_swap(weight, 1)
        docs = after(docs, cross0)
    (info,) = call(
        limits_kernel,
        [((parts, 8, ROWS), jnp.int32)],
        [], 4, 1,
        docs,
    )
    query_stack = stack_heads(queries, head)
    grad_stack = stack_heads(grad_out, head)
    mine = [fan_out(after(keys, info), k) for k in steps]
    other = [core_swap(after(block, z1, z2) if direct else block) for block in mine]

    if direct:
        cross = [cross0] + [dp_swap(block, 1) for block in (z1, z2, z3)]
        info = after(info, *cross[:3])

    probs, key_window, own_v, mine_v, give_v = call(
        weights_kernel,
        [
            ((parts, chunks, CHUNK, stack), BF16),
            ((window, head), BF16),
            ((rows, head), F32),
            ((SPAN, rows, head), F32),
            ((SPAN, rows, head), BF16),
        ],
        [
            pltpu.VMEM((chunks, CHUNK, stack), F32),
            pltpu.VMEM((window, head), F32),
        ],
        20, 0,
        info, query_stack, grad_stack, keys, *mine, *other,
    )
    got_v = core_swap(give_v)
    other_v = core_swap(own_v)

    if direct:
        value_part, full_weight = call(
            value_kernel,
            [((rows, head), F32), ((head, depth), BF16)],
            [], 12, 0,
            layer_input, weight, z1, z2, z3, *cross,
        )
    else:
        full_weight = lax.all_gather(weight, "dp", axis=0, tiled=True)
        value_part = nt_dot(layer_input, full_weight)
    value, *packs = call(
        pack_kernel,
        [((rows, head), BF16)] + [((2, rows, head), BF16)] * SPAN,
        [], 8, 0,
        value_part, core_swap(value_part), mine_v, got_v,
    )
    mine = [fan_out(pack, k) for pack, k in zip(packs, steps)]
    other = [core_swap(block) for block in mine]

    if direct:
        grad_value, *blocks = call(
            weight_grad_kernel,
            [((rows, head), BF16)] + [((width, depth), F32)] * 4 + [((width, depth), BF16)] * 4,
            [pltpu.VMEM((head, depth), F32)], 16, 0,
            layer_input, own_v, other_v, *mine, *other,
        )
        keep, send = blocks[:4], blocks[4:]
        total = keep[0]
        for k in (3, 2, 1):
            pair = (keep[k] + dp_swap(send[k], 1).astype(F32)).astype(BF16)
            total = total + dp_swap(pair, 2 * k).astype(F32)
        total = total + dp_swap(send[0], 1).astype(F32)
        grad_weight = total.T
    else:
        grad_value = sum_blocks(
            own_v, other_v, [block[1] for block in mine], [block[1] for block in other]
        ).astype(BF16)
        grad_weight = lax.psum_scatter(
            tn_dot(grad_value, layer_input), "dp", scatter_dimension=0, tiled=True
        ).T
    grad_stack_q, own_k, mine_k, give_k = call(
        scores_kernel,
        [
            ((parts, head, stack), F32),
            ((rows, head), F32),
            ((SPAN, rows, head), F32),
            ((SPAN, rows, head), BF16),
        ],
        [
            pltpu.VMEM((window, head), BF16),
            pltpu.VMEM((chunks, CHUNK, stack), F32),
            pltpu.VMEM((window, head), F32),
        ],
        20, 0,
        after(info, grad_value), query_stack, grad_stack, probs, key_window, value, *mine, *other,
    )
    got_k = core_swap(give_k)
    mine = [
        fan_out((mine_k[k] + got_k[k].astype(F32)).astype(BF16), k) for k in steps
    ]
    other = [core_swap(block) for block in mine]
    grad_input, grad_queries = call(
        finish_kernel,
        [((rows, depth), BF16), ((rows, heads * head), BF16)],
        [
            pltpu.VMEM((rows, depth), BF16),
            pltpu.VMEM((rows, heads * head), BF16),
            pltpu.SemaphoreType.DMA((9,)),
        ],
        12, 0,
        grad_value, full_weight, grad_stack_q,
    )
    grad_keys = sum_blocks(own_k, core_swap(own_k), mine, other).astype(BF16)
    return (grad_input, grad_queries, grad_keys, grad_weight)


def solution(mesh):
    in_specs = (
        P(("groups", "dp"), "fsdp"),
        P("fsdp", "dp"),
        P(("groups", "dp"), "fsdp"),
        P(("groups", "dp"), None),
        P(("groups", "dp"), "fsdp"),
        P("groups"),
        P("groups"),
    )
    out_specs = (
        P(("groups", "dp"), "fsdp"),
        P(("groups", "dp"), "fsdp"),
        P(("groups", "dp"), None),
        P(("groups", "fsdp"), "dp"),
    )
    return jax.shard_map(body, mesh=mesh, in_specs=in_specs, out_specs=out_specs, check_vma=False)
```

```python
import math

import jax
import jax.numpy as jnp
from jax import lax
from jax.experimental import pallas as pl
from jax.experimental.pallas import tpu as pltpu
from jax.sharding import PartitionSpec as P

SPAN = 3
NEGATIVE = -1e30
CHUNK = 256
ROWS = 128
BOTH = ("dp", "fsdp")
F32 = jnp.float32
BF16 = jnp.bfloat16
VMEM = pl.BlockSpec(memory_space=pltpu.VMEM)
SMEM = pl.BlockSpec(memory_space=pltpu.SMEM)
HBM = pl.BlockSpec(memory_space=pl.ANY)


def core_swap(value):
    return lax.ppermute(value, "fsdp", [(0, 1), (1, 0)])


def dp_swap(value, mask):
    count = lax.axis_size("dp")
    return lax.ppermute(value, "dp", [(i, i ^ mask) for i in range(count)])


def partner(step, me):
    turn = 1 - 2 * (me % 2)
    row = 2 - 4 * ((me // 2) % 2)
    return ((-3 * turn, 3 * turn), (row, -turn), (-row, turn))[step]


def offset(step, core):
    near, there = partner(step, lax.axis_index("dp"))
    return jnp.where(core == 0, near, there)


def fan_out(value, step):
    count = lax.axis_size("dp")
    pairs = [(2 * i + c, 2 * (i + partner(step, i)[c]) + c) for i in range(count) for c in (0, 1)]
    return lax.ppermute(value, BOTH, [(i, j) for i, j in pairs if 0 <= j < 2 * count])


def after(value, *others):
    return lax.optimization_barrier((value, *others))[0]


def chunk_range(first, window_first, docs_ref):
    last = first + ROWS - 1
    zero = jnp.int32(0)
    count = docs_ref.shape[0] // 2
    position = first + lax.broadcasted_iota(jnp.int32, (1, ROWS), 1)
    low, high = jnp.zeros((1, ROWS), jnp.int32), jnp.zeros((1, ROWS), jnp.int32)

    def step(doc, carry):
        start, least, most, low, high = carry
        length = docs_ref[doc]
        end = start + length
        bound = start + jnp.minimum(docs_ref[count + doc], length)
        least = jnp.where((start <= first) & (first < end), start, least)
        most = jnp.where((start <= last) & (last < end), jnp.maximum(last + 1, bound), most)
        inside = (position >= start) & (position < end)
        low = jnp.where(inside, start, low)
        high = jnp.where(inside, jnp.maximum(position + 1, bound), high)
        return (end, least, most, low, high)

    carry = (zero, zero, zero, low, high)
    if count <= 8:
        for doc in range(count):
            carry = step(doc, carry)
    else:
        carry = lax.fori_loop(0, count, step, carry)
    _, least, most, low, high = carry
    chunk_low = lax.div(least - window_first, CHUNK)
    chunk_high = lax.div(most - window_first + CHUNK - 1, CHUNK)
    return chunk_low, chunk_high, low, high


def at_block(index, rows):
    return pl.ds(pl.multiple_of(index * rows, rows), rows)


def place_window(core, window_ref, own, mine, other):
    rows = own.shape[0]
    window_ref[SPAN * rows : (SPAN + 1) * rows, :] = own
    for k in range(SPAN):
        window_ref[at_block(SPAN + offset(k, core), rows), :] = mine[k]
        window_ref[at_block(SPAN + offset(k, 1 - core), rows), :] = other[k]


def give_out(core, total_ref, own_ref, mine_ref, give_ref, factor):
    rows = own_ref.shape[0]
    own_ref[...] = total_ref[SPAN * rows : (SPAN + 1) * rows, :] * factor
    for k in range(SPAN):
        mine_ref[k] = total_ref[at_block(SPAN + offset(k, core), rows), :] * factor
        there = total_ref[at_block(SPAN + offset(k, 1 - core), rows), :] * factor
        give_ref[k] = there.astype(BF16)


def stack_heads(value, head):
    rows, wide = value.shape
    split = value.reshape(rows // ROWS, ROWS, wide // head, head)
    return split.transpose(0, 2, 1, 3).reshape(rows // ROWS, -1, head)


def nt_dot(a, b):
    return lax.dot_general(a, b, (((1,), (1,)), ((), ())), preferred_element_type=F32)


def tn_dot(a, b):
    return lax.dot_general(a, b, (((0,), (0,)), ((), ())), preferred_element_type=F32)


def fold(total, value, reduce):
    rows, lanes = value.shape
    return reduce(jnp.concatenate([total[None], value.reshape(rows // 8, 8, lanes)]), axis=0)


def limits_kernel(docs_ref, info_ref):
    rows = info_ref.shape[0] * ROWS
    first = lax.axis_index("dp") * rows
    window_first = first - SPAN * rows
    info_ref[...] = jnp.zeros_like(info_ref)
    for part in range(rows // ROWS):
        chunk_low, chunk_high, low, high = chunk_range(
            first + part * ROWS, window_first, docs_ref
        )
        info_ref[part, 0:1] = low - window_first
        info_ref[part, 1:2] = high - window_first
        info_ref[part, 2:3] = jnp.zeros_like(low) + chunk_low
        info_ref[part, 3:4] = jnp.zeros_like(low) + (chunk_high - chunk_low)


def by_count(count, most, body):
    for n in range(1, most + 1):

        @pl.when(count == n)
        def _():
            body(n)


def weights_kernel(
    info_ref, queries_ref, grads_ref, key_ref, r1, r2, r3, s1, s2, s3,
    probs_ref, window_ref, own_ref, mine_ref, give_ref,
    score_ref, total_ref,
):
    rows = key_ref.shape[0]
    stack = queries_ref.shape[1]
    core = lax.axis_index("fsdp")
    place_window(
        core, window_ref, key_ref[...], (r1[...], r2[...], r3[...]), (s1[...], s2[...], s3[...])
    )
    total_ref[...] = jnp.zeros_like(total_ref)
    power = math.log2(math.e) / math.sqrt(128.0)
    index = lax.broadcasted_iota(jnp.int32, (CHUNK, ROWS), 0)

    def part_step(part):
        chunk_low = info_ref[part, 2:3][0, 0]
        low = info_ref[part, 0:1] - chunk_low * CHUNK
        high = info_ref[part, 1:2] - chunk_low * CHUNK

        def chunks(count):
            peak = jnp.full((8, stack), NEGATIVE, F32)
            for i in range(count):
                scores = nt_dot(window_ref[at_block(chunk_low + i, CHUNK), :], queries_ref[part])
                place = index + i * CHUNK
                seen = (place >= low) & (place < high)
                seen = jnp.concatenate([seen] * (stack // ROWS), axis=1)
                masked = jnp.where(seen, scores, NEGATIVE)
                score_ref[i] = masked
                peak = fold(peak, masked, jnp.max)
            peak = jnp.max(peak, axis=0, keepdims=True)
            total = jnp.zeros((8, stack), F32)
            for i in range(count):
                probs = jnp.exp2((score_ref[i] - peak) * power)
                score_ref[i] = probs
                total = fold(total, probs, jnp.sum)
            inverse = 1.0 / jnp.sum(total, axis=0, keepdims=True)
            for i in range(count):
                probs = (score_ref[i] * inverse).astype(BF16)
                probs_ref[part, i] = probs
                total_ref[at_block(chunk_low + i, CHUNK), :] += jnp.dot(
                    probs, grads_ref[part], preferred_element_type=F32
                )

        by_count(info_ref[part, 3:4][0, 0], probs_ref.shape[1], chunks)

    for part in range(rows // ROWS):
        part_step(part)
    give_out(core, total_ref, own_ref, mine_ref, give_ref, 1.0)


def scores_kernel(
    info_ref, queries_ref, grads_ref, probs_ref, keys_ref, value_ref,
    r1, r2, r3, s1, s2, s3,
    query_ref, own_ref, mine_ref, give_ref,
    values_ref, product_ref, total_ref,
):
    rows = value_ref.shape[0]
    stack = queries_ref.shape[1]
    core = lax.axis_index("fsdp")
    place_window(core, values_ref, value_ref[...], (r1[0], r2[0], r3[0]), (s1[0], s2[0], s3[0]))
    total_ref[...] = jnp.zeros_like(total_ref)
    scaling = 1.0 / math.sqrt(128.0)

    def part_step(part, _):
        chunk_low = info_ref[part, 2:3][0, 0]

        def chunks(count):
            delta = jnp.zeros((8, stack), F32)
            for i in range(count):
                product = nt_dot(values_ref[at_block(chunk_low + i, CHUNK), :], grads_ref[part])
                product_ref[i] = product
                delta = fold(delta, product * probs_ref[part, i].astype(F32), jnp.sum)
            delta = jnp.sum(delta, axis=0, keepdims=True)
            query = jnp.zeros(query_ref.shape[1:], F32)
            for i in range(count):
                at = at_block(chunk_low + i, CHUNK)
                grad = (probs_ref[part, i].astype(F32) * (product_ref[i] - delta)).astype(BF16)
                total_ref[at, :] += jnp.dot(grad, queries_ref[part], preferred_element_type=F32)
                query += tn_dot(keys_ref[at, :], grad)
            query_ref[part] = query * scaling

        by_count(info_ref[part, 3:4][0, 0], probs_ref.shape[1], chunks)
        return 0

    lax.fori_loop(0, rows // ROWS, part_step, 0)
    give_out(core, total_ref, own_ref, mine_ref, give_ref, scaling)


def pack_kernel(half_ref, other_ref, mine_ref, got_ref, value_ref, *outs):
    value = (half_ref[...] + other_ref[...]).astype(BF16)
    value_ref[...] = value
    for k, out in enumerate(outs):
        out[0] = value
        out[1] = (mine_ref[k] + got_ref[k].astype(F32)).astype(BF16)


def sum_blocks(own, other, mine, others):
    total = own + other
    for a, b in zip(mine, others):
        total = total + (a.astype(F32) + b.astype(F32))
    return total


def value_kernel(x_ref, z0, z1, z2, z3, c0, c1, c2, c3, part_ref, weight_ref):
    me = lax.axis_index("dp")
    width = z0.shape[0]
    for k, (near, cross) in enumerate(((z0, c0), (z1, c1), (z2, c2), (z3, c3))):
        owner = me ^ (2 * k)
        weight_ref[pl.ds(pl.multiple_of(owner * width, width), width), :] = near[...]
        there = owner ^ 1
        weight_ref[pl.ds(pl.multiple_of(there * width, width), width), :] = cross[...]
    part_ref[...] = nt_dot(x_ref[...], weight_ref[...])


def weight_grad_kernel(x_ref, a_ref, b_ref, r1, r2, r3, s1, s2, s3, grad_ref, *outs):
    me = lax.axis_index("dp")
    grad = sum_blocks(
        a_ref[...], b_ref[...], (r1[1], r2[1], r3[1]), (s1[1], s2[1], s3[1])
    ).astype(BF16)
    grad_ref[...] = grad
    depth = x_ref.shape[1]
    width = outs[0].shape[0]
    step = 512
    scratch = outs[8]
    for at in range(0, depth, step):
        scratch[:, at : at + step] = tn_dot(grad, x_ref[:, at : at + step])
    for k in range(4):
        owner = me ^ (2 * k)
        outs[k][...] = scratch[pl.ds(pl.multiple_of(owner * width, width), width), :]
        there = owner ^ 1
        rows = scratch[pl.ds(pl.multiple_of(there * width, width), width), :]
        outs[4 + k][...] = rows.astype(BF16)


def finish_kernel(grad_ref, weight_ref, query_ref, out_hbm, query_hbm, out_ref, turned_ref, sems):
    copies = []
    for part in range(query_ref.shape[0]):
        for h in range(0, query_ref.shape[2], ROWS):
            turned_ref[part * ROWS : (part + 1) * ROWS, h : h + ROWS] = (
                query_ref[part, :, h : h + ROWS].T.astype(BF16)
            )
    copies.append(pltpu.make_async_copy(turned_ref, query_hbm, sems.at[8]))
    copies[-1].start()
    step = out_ref.shape[1] // 8
    for i in range(8):
        cut = slice(i * step, (i + 1) * step)
        out_ref[:, cut] = jnp.dot(
            grad_ref[...], weight_ref[:, cut], preferred_element_type=F32
        ).astype(BF16)
        copies.append(
            pltpu.make_async_copy(out_ref.at[:, cut], out_hbm.at[:, cut], sems.at[i])
        )
        copies[-1].start()
    for copy in copies:
        copy.wait()


def call(kernel, outs, scratch, limit_mib, smem, *args):
    return pl.pallas_call(
        kernel,
        in_specs=[SMEM] * smem + [VMEM] * (len(args) - smem),
        out_specs=[HBM if kernel is finish_kernel else VMEM for _ in outs],
        out_shape=[jax.ShapeDtypeStruct(shape, kind) for shape, kind in outs],
        scratch_shapes=scratch,
        compiler_params=pltpu.CompilerParams(vmem_limit_bytes=limit_mib << 20),
        cost_estimate=pl.CostEstimate(flops=1 << 30, bytes_accessed=4 << 20, transcendentals=0),
    )(*args)


def body(layer_input, w_value, queries, keys, grad_out, doc_lengths, prefix_spans):
    rows, depth = layer_input.shape
    head = keys.shape[1]
    heads = queries.shape[1] // head
    dp = lax.axis_size("dp")
    window = (2 * SPAN + 1) * rows
    chunks = window // CHUNK
    parts = rows // ROWS
    stack = heads * ROWS
    weight = w_value.T
    width = weight.shape[0]
    direct = dp == 8
    steps = range(SPAN)

    docs = jnp.concatenate([doc_lengths, prefix_spans])
    if direct:
        z3, z2, z1 = (dp_swap(weight, 2 * k) for k in (3, 2, 1))
        cross0 = dp_swap(weight, 1)
        docs = after(docs, cross0)
    (info,) = call(
        limits_kernel,
        [((parts, 8, ROWS), jnp.int32)],
        [], 4, 1,
        docs,
    )
    query_stack = stack_heads(queries, head)
    grad_stack = stack_heads(grad_out, head)
    mine = [fan_out(after(keys, info), k) for k in steps]
    other = [core_swap(after(block, z1, z2) if direct else block) for block in mine]

    if direct:
        cross = [cross0] + [dp_swap(block, 1) for block in (z1, z2, z3)]
        info = after(info, *cross[:3])

    probs, key_window, own_v, mine_v, give_v = call(
        weights_kernel,
        [
            ((parts, chunks, CHUNK, stack), BF16),
            ((window, head), BF16),
            ((rows, head), F32),
            ((SPAN, rows, head), F32),
            ((SPAN, rows, head), BF16),
        ],
        [
            pltpu.VMEM((chunks, CHUNK, stack), F32),
            pltpu.VMEM((window, head), F32),
        ],
        20, 0,
        info, query_stack, grad_stack, keys, *mine, *other,
    )
    got_v = core_swap(give_v)
    other_v = core_swap(own_v)

    if direct:
        value_part, full_weight = call(
            value_kernel,
            [((rows, head), F32), ((head, depth), BF16)],
            [], 12, 0,
            layer_input, weight, z1, z2, z3, *cross,
        )
    else:
        full_weight = lax.all_gather(weight, "dp", axis=0, tiled=True)
        value_part = nt_dot(layer_input, full_weight)
    value, *packs = call(
        pack_kernel,
        [((rows, head), BF16)] + [((2, rows, head), BF16)] * SPAN,
        [], 8, 0,
        value_part, core_swap(value_part), mine_v, got_v,
    )
    mine = [fan_out(pack, k) for pack, k in zip(packs, steps)]
    other = [core_swap(block) for block in mine]

    if direct:
        grad_value, *blocks = call(
            weight_grad_kernel,
            [((rows, head), BF16)] + [((width, depth), F32)] * 4 + [((width, depth), BF16)] * 4,
            [pltpu.VMEM((head, depth), F32)], 16, 0,
            layer_input, own_v, other_v, *mine, *other,
        )
        keep, send = blocks[:4], blocks[4:]
        total = keep[0]
        for k in (3, 2, 1):
            pair = (keep[k] + dp_swap(send[k], 1).astype(F32)).astype(BF16)
            total = total + dp_swap(pair, 2 * k).astype(F32)
        total = total + dp_swap(send[0], 1).astype(F32)
        grad_weight = total.T
    else:
        grad_value = sum_blocks(
            own_v, other_v, [block[1] for block in mine], [block[1] for block in other]
        ).astype(BF16)
        grad_weight = lax.psum_scatter(
            tn_dot(grad_value, layer_input), "dp", scatter_dimension=0, tiled=True
        ).T
    grad_stack_q, own_k, mine_k, give_k = call(
        scores_kernel,
        [
            ((parts, head, stack), F32),
            ((rows, head), F32),
            ((SPAN, rows, head), F32),
            ((SPAN, rows, head), BF16),
        ],
        [
            pltpu.VMEM((window, head), BF16),
            pltpu.VMEM((chunks, CHUNK, stack), F32),
            pltpu.VMEM((window, head), F32),
        ],
        20, 0,
        after(info, grad_value), query_stack, grad_stack, probs, key_window, value, *mine, *other,
    )
    got_k = core_swap(give_k)
    mine = [
        fan_out((mine_k[k] + got_k[k].astype(F32)).astype(BF16), k) for k in steps
    ]
    other = [core_swap(block) for block in mine]
    grad_input, grad_queries = call(
        finish_kernel,
        [((rows, depth), BF16), ((rows, heads * head), BF16)],
        [
            pltpu.VMEM((rows, depth), BF16),
            pltpu.VMEM((rows, heads * head), BF16),
            pltpu.SemaphoreType.DMA((9,)),
        ],
        12, 0,
        grad_value, full_weight, grad_stack_q,
    )
    grad_keys = sum_blocks(own_k, core_swap(own_k), mine, other).astype(BF16)
    return (grad_input, grad_queries, grad_keys, grad_weight)


def solution(mesh):
    in_specs = (
        P(("groups", "dp"), "fsdp"),
        P("fsdp", "dp"),
        P(("groups", "dp"), "fsdp"),
        P(("groups", "dp"), None),
        P(("groups", "dp"), "fsdp"),
        P("groups"),
        P("groups"),
    )
    out_specs = (
        P(("groups", "dp"), "fsdp"),
        P(("groups", "dp"), "fsdp"),
        P(("groups", "dp"), None),
        P(("groups", "fsdp"), "dp"),
    )
    return jax.shard_map(body, mesh=mesh, in_specs=in_specs, out_specs=out_specs, check_vma=False)
```

```python
import math

import jax
import jax.numpy as jnp
from jax import lax
from jax.experimental import pallas as pl
from jax.experimental.pallas import tpu as pltpu
from jax.sharding import PartitionSpec as P

SPAN = 3
NEGATIVE = -1e30
CHUNK = 256
ROWS = 128
BOTH = ("dp", "fsdp")
F32 = jnp.float32
BF16 = jnp.bfloat16
VMEM = pl.BlockSpec(memory_space=pltpu.VMEM)
SMEM = pl.BlockSpec(memory_space=pltpu.SMEM)
HBM = pl.BlockSpec(memory_space=pl.ANY)


def core_swap(value):
    return lax.ppermute(value, "fsdp", [(0, 1), (1, 0)])


def dp_swap(value, mask):
    count = lax.axis_size("dp")
    return lax.ppermute(value, "dp", [(i, i ^ mask) for i in range(count)])


def partner(step, me):
    turn = 1 - 2 * (me % 2)
    row = 2 - 4 * ((me // 2) % 2)
    return ((row, turn), (-row, -turn), (-3 * turn, 3 * turn))[step]


def offset(step, core):
    near, there = partner(step, lax.axis_index("dp"))
    return jnp.where(core == 0, near, there)


def fan_out(value, step):
    count = lax.axis_size("dp")
    pairs = [(2 * i + c, 2 * (i + partner(step, i)[c]) + c) for i in range(count) for c in (0, 1)]
    return lax.ppermute(value, BOTH, [(i, j) for i, j in pairs if 0 <= j < 2 * count])


def after(value, *others):
    return lax.optimization_barrier((value, *others))[0]


def chunk_range(first, window_first, docs_ref):
    last = first + ROWS - 1
    zero = jnp.int32(0)
    count = docs_ref.shape[0] // 2
    position = first + lax.broadcasted_iota(jnp.int32, (1, ROWS), 1)
    low, high = jnp.zeros((1, ROWS), jnp.int32), jnp.zeros((1, ROWS), jnp.int32)

    def step(doc, carry):
        start, least, most, low, high = carry
        length = docs_ref[doc]
        end = start + length
        bound = start + jnp.minimum(docs_ref[count + doc], length)
        least = jnp.where((start <= first) & (first < end), start, least)
        most = jnp.where((start <= last) & (last < end), jnp.maximum(last + 1, bound), most)
        inside = (position >= start) & (position < end)
        low = jnp.where(inside, start, low)
        high = jnp.where(inside, jnp.maximum(position + 1, bound), high)
        return (end, least, most, low, high)

    carry = (zero, zero, zero, low, high)
    if count <= 8:
        for doc in range(count):
            carry = step(doc, carry)
    else:
        carry = lax.fori_loop(0, count, step, carry)
    _, least, most, low, high = carry
    chunk_low = lax.div(least - window_first, CHUNK)
    chunk_high = lax.div(most - window_first + CHUNK - 1, CHUNK)
    return chunk_low, chunk_high, low, high


def at_block(index, rows):
    return pl.ds(pl.multiple_of(index * rows, rows), rows)


def place_window(core, window_ref, own, mine, other):
    rows = own.shape[0]
    window_ref[SPAN * rows : (SPAN + 1) * rows, :] = own
    for k in range(SPAN):
        window_ref[at_block(SPAN + offset(k, core), rows), :] = mine[k]
        window_ref[at_block(SPAN + offset(k, 1 - core), rows), :] = other[k]


def give_out(core, total_ref, own_ref, mine_ref, give_ref, factor):
    rows = own_ref.shape[0]
    own_ref[...] = total_ref[SPAN * rows : (SPAN + 1) * rows, :] * factor
    for k in range(SPAN):
        mine_ref[k] = total_ref[at_block(SPAN + offset(k, core), rows), :] * factor
        there = total_ref[at_block(SPAN + offset(k, 1 - core), rows), :] * factor
        give_ref[k] = there.astype(BF16)


def stack_heads(value, head):
    rows, wide = value.shape
    split = value.reshape(rows // ROWS, ROWS, wide // head, head)
    return split.transpose(0, 2, 1, 3).reshape(rows // ROWS, -1, head)


def nt_dot(a, b):
    return lax.dot_general(a, b, (((1,), (1,)), ((), ())), preferred_element_type=F32)


def tn_dot(a, b):
    return lax.dot_general(a, b, (((0,), (0,)), ((), ())), preferred_element_type=F32)


def fold(total, value, reduce):
    rows, lanes = value.shape
    return reduce(jnp.concatenate([total[None], value.reshape(rows // 8, 8, lanes)]), axis=0)


def limits_kernel(docs_ref, info_ref):
    rows = info_ref.shape[0] * ROWS
    first = lax.axis_index("dp") * rows
    window_first = first - SPAN * rows
    info_ref[...] = jnp.zeros_like(info_ref)
    for part in range(rows // ROWS):
        chunk_low, chunk_high, low, high = chunk_range(
            first + part * ROWS, window_first, docs_ref
        )
        info_ref[part, 0:1] = low - window_first
        info_ref[part, 1:2] = high - window_first
        info_ref[part, 2:3] = jnp.zeros_like(low) + chunk_low
        info_ref[part, 3:4] = jnp.zeros_like(low) + (chunk_high - chunk_low)


def by_count(count, most, body):
    for n in range(1, most + 1):

        @pl.when(count == n)
        def _():
            body(n)


def weights_kernel(
    info_ref, queries_ref, grads_ref, key_ref, r1, r2, r3, s1, s2, s3,
    probs_ref, window_ref, own_ref, mine_ref, give_ref,
    score_ref, total_ref,
):
    rows = key_ref.shape[0]
    stack = queries_ref.shape[1]
    core = lax.axis_index("fsdp")
    place_window(
        core, window_ref, key_ref[...], (r1[...], r2[...], r3[...]), (s1[...], s2[...], s3[...])
    )
    total_ref[...] = jnp.zeros_like(total_ref)
    power = math.log2(math.e) / math.sqrt(128.0)
    index = lax.broadcasted_iota(jnp.int32, (CHUNK, ROWS), 0)

    def part_step(part):
        chunk_low = info_ref[part, 2:3][0, 0]
        low = info_ref[part, 0:1] - chunk_low * CHUNK
        high = info_ref[part, 1:2] - chunk_low * CHUNK

        def chunks(count):
            peak = jnp.full((8, stack), NEGATIVE, F32)
            for i in range(count):
                scores = nt_dot(window_ref[at_block(chunk_low + i, CHUNK), :], queries_ref[part])
                place = index + i * CHUNK
                seen = (place >= low) & (place < high)
                seen = jnp.concatenate([seen] * (stack // ROWS), axis=1)
                masked = jnp.where(seen, scores, NEGATIVE)
                score_ref[i] = masked
                peak = fold(peak, masked, jnp.max)
            peak = jnp.max(peak, axis=0, keepdims=True)
            total = jnp.zeros((8, stack), F32)
            for i in range(count):
                probs = jnp.exp2((score_ref[i] - peak) * power)
                score_ref[i] = probs
                total = fold(total, probs, jnp.sum)
            inverse = 1.0 / jnp.sum(total, axis=0, keepdims=True)
            for i in range(count):
                probs = (score_ref[i] * inverse).astype(BF16)
                probs_ref[part, i] = probs
                total_ref[at_block(chunk_low + i, CHUNK), :] += jnp.dot(
                    probs, grads_ref[part], preferred_element_type=F32
                )

        by_count(info_ref[part, 3:4][0, 0], probs_ref.shape[1], chunks)

    for part in range(rows // ROWS):
        part_step(part)
    give_out(core, total_ref, own_ref, mine_ref, give_ref, 1.0)


def scores_kernel(
    info_ref, queries_ref, grads_ref, probs_ref, keys_ref, value_ref,
    r1, r2, r3, s1, s2, s3,
    query_ref, own_ref, mine_ref, give_ref,
    values_ref, product_ref, total_ref,
):
    rows = value_ref.shape[0]
    stack = queries_ref.shape[1]
    core = lax.axis_index("fsdp")
    place_window(core, values_ref, value_ref[...], (r1[0], r2[0], r3[0]), (s1[0], s2[0], s3[0]))
    total_ref[...] = jnp.zeros_like(total_ref)
    scaling = 1.0 / math.sqrt(128.0)

    def part_step(part, _):
        chunk_low = info_ref[part, 2:3][0, 0]

        def chunks(count):
            delta = jnp.zeros((8, stack), F32)
            for i in range(count):
                product = nt_dot(values_ref[at_block(chunk_low + i, CHUNK), :], grads_ref[part])
                product_ref[i] = product
                delta = fold(delta, product * probs_ref[part, i].astype(F32), jnp.sum)
            delta = jnp.sum(delta, axis=0, keepdims=True)
            query = jnp.zeros(query_ref.shape[1:], F32)
            for i in range(count):
                at = at_block(chunk_low + i, CHUNK)
                grad = (probs_ref[part, i].astype(F32) * (product_ref[i] - delta)).astype(BF16)
                total_ref[at, :] += jnp.dot(grad, queries_ref[part], preferred_element_type=F32)
                query += tn_dot(keys_ref[at, :], grad)
            query_ref[part] = query * scaling

        by_count(info_ref[part, 3:4][0, 0], probs_ref.shape[1], chunks)
        return 0

    lax.fori_loop(0, rows // ROWS, part_step, 0)
    give_out(core, total_ref, own_ref, mine_ref, give_ref, scaling)


def pack_kernel(half_ref, other_ref, mine_ref, got_ref, value_ref, *outs):
    value = (half_ref[...] + other_ref[...]).astype(BF16)
    value_ref[...] = value
    for k, out in enumerate(outs):
        out[0] = value
        out[1] = (mine_ref[k] + got_ref[k].astype(F32)).astype(BF16)


def sum_blocks(own, other, mine, others):
    total = own + other
    for a, b in zip(mine, others):
        total = total + (a.astype(F32) + b.astype(F32))
    return total


def value_kernel(x_ref, z0, z1, z2, z3, c0, c1, c2, c3, part_ref, weight_ref):
    me = lax.axis_index("dp")
    width = z0.shape[0]
    for k, (near, cross) in enumerate(((z0, c0), (z1, c1), (z2, c2), (z3, c3))):
        owner = me ^ (2 * k)
        weight_ref[pl.ds(pl.multiple_of(owner * width, width), width), :] = near[...]
        there = owner ^ 1
        weight_ref[pl.ds(pl.multiple_of(there * width, width), width), :] = cross[...]
    part_ref[...] = nt_dot(x_ref[...], weight_ref[...])


def weight_grad_kernel(x_ref, a_ref, b_ref, r1, r2, r3, s1, s2, s3, grad_ref, *outs):
    me = lax.axis_index("dp")
    grad = sum_blocks(
        a_ref[...], b_ref[...], (r1[1], r2[1], r3[1]), (s1[1], s2[1], s3[1])
    ).astype(BF16)
    grad_ref[...] = grad
    depth = x_ref.shape[1]
    width = outs[0].shape[0]
    step = 512
    scratch = outs[8]
    for at in range(0, depth, step):
        scratch[:, at : at + step] = tn_dot(grad, x_ref[:, at : at + step])
    for k in range(4):
        owner = me ^ (2 * k)
        outs[k][...] = scratch[pl.ds(pl.multiple_of(owner * width, width), width), :]
        there = owner ^ 1
        rows = scratch[pl.ds(pl.multiple_of(there * width, width), width), :]
        outs[4 + k][...] = rows.astype(BF16)


def finish_kernel(grad_ref, weight_ref, query_ref, out_hbm, query_hbm, out_ref, turned_ref, sems):
    copies = []
    for part in range(query_ref.shape[0]):
        for h in range(0, query_ref.shape[2], ROWS):
            turned_ref[part * ROWS : (part + 1) * ROWS, h : h + ROWS] = (
                query_ref[part, :, h : h + ROWS].T.astype(BF16)
            )
    copies.append(pltpu.make_async_copy(turned_ref, query_hbm, sems.at[8]))
    copies[-1].start()
    step = out_ref.shape[1] // 8
    for i in range(8):
        cut = slice(i * step, (i + 1) * step)
        out_ref[:, cut] = jnp.dot(
            grad_ref[...], weight_ref[:, cut], preferred_element_type=F32
        ).astype(BF16)
        copies.append(
            pltpu.make_async_copy(out_ref.at[:, cut], out_hbm.at[:, cut], sems.at[i])
        )
        copies[-1].start()
    for copy in copies:
        copy.wait()


def call(kernel, outs, scratch, limit_mib, smem, *args):
    return pl.pallas_call(
        kernel,
        in_specs=[SMEM] * smem + [VMEM] * (len(args) - smem),
        out_specs=[HBM if kernel is finish_kernel else VMEM for _ in outs],
        out_shape=[jax.ShapeDtypeStruct(shape, kind) for shape, kind in outs],
        scratch_shapes=scratch,
        compiler_params=pltpu.CompilerParams(vmem_limit_bytes=limit_mib << 20),
        cost_estimate=pl.CostEstimate(flops=1 << 30, bytes_accessed=4 << 20, transcendentals=0),
    )(*args)


def body(layer_input, w_value, queries, keys, grad_out, doc_lengths, prefix_spans):
    rows, depth = layer_input.shape
    head = keys.shape[1]
    heads = queries.shape[1] // head
    dp = lax.axis_size("dp")
    window = (2 * SPAN + 1) * rows
    chunks = window // CHUNK
    parts = rows // ROWS
    stack = heads * ROWS
    weight = w_value.T
    width = weight.shape[0]
    direct = dp == 8
    steps = range(SPAN)

    docs = jnp.concatenate([doc_lengths, prefix_spans])
    if direct:
        z3, z2, z1 = (dp_swap(weight, 2 * k) for k in (3, 2, 1))
        cross0 = dp_swap(weight, 1)
        docs = after(docs, cross0)
    (info,) = call(
        limits_kernel,
        [((parts, 8, ROWS), jnp.int32)],
        [], 4, 1,
        docs,
    )
    query_stack = stack_heads(queries, head)
    grad_stack = stack_heads(grad_out, head)
    mine = [fan_out(after(keys, info), k) for k in steps]
    other = [core_swap(after(block, z1, z2) if direct else block) for block in mine]

    if direct:
        cross = [cross0] + [dp_swap(block, 1) for block in (z1, z2, z3)]
        info = after(info, *cross[:3])

    probs, key_window, own_v, mine_v, give_v = call(
        weights_kernel,
        [
            ((parts, chunks, CHUNK, stack), BF16),
            ((window, head), BF16),
            ((rows, head), F32),
            ((SPAN, rows, head), F32),
            ((SPAN, rows, head), BF16),
        ],
        [
            pltpu.VMEM((chunks, CHUNK, stack), F32),
            pltpu.VMEM((window, head), F32),
        ],
        20, 0,
        info, query_stack, grad_stack, keys, *mine, *other,
    )
    got_v = core_swap(give_v)
    other_v = core_swap(own_v)

    if direct:
        value_part, full_weight = call(
            value_kernel,
            [((rows, head), F32), ((head, depth), BF16)],
            [], 12, 0,
            layer_input, weight, z1, z2, z3, *cross,
        )
    else:
        full_weight = lax.all_gather(weight, "dp", axis=0, tiled=True)
        value_part = nt_dot(layer_input, full_weight)
    value, *packs = call(
        pack_kernel,
        [((rows, head), BF16)] + [((2, rows, head), BF16)] * SPAN,
        [], 8, 0,
        value_part, core_swap(value_part), mine_v, got_v,
    )
    mine = [fan_out(pack, k) for pack, k in zip(packs, steps)]
    other = [core_swap(block) for block in mine]

    if direct:
        grad_value, *blocks = call(
            weight_grad_kernel,
            [((rows, head), BF16)] + [((width, depth), F32)] * 4 + [((width, depth), BF16)] * 4,
            [pltpu.VMEM((head, depth), F32)], 16, 0,
            layer_input, own_v, other_v, *mine, *other,
        )
        keep, send = blocks[:4], blocks[4:]
        total = keep[0]
        for k in (3, 2, 1):
            pair = (keep[k] + dp_swap(send[k], 1).astype(F32)).astype(BF16)
            total = total + dp_swap(pair, 2 * k).astype(F32)
        total = total + dp_swap(send[0], 1).astype(F32)
        grad_weight = total.T
    else:
        grad_value = sum_blocks(
            own_v, other_v, [block[1] for block in mine], [block[1] for block in other]
        ).astype(BF16)
        grad_weight = lax.psum_scatter(
            tn_dot(grad_value, layer_input), "dp", scatter_dimension=0, tiled=True
        ).T
    grad_stack_q, own_k, mine_k, give_k = call(
        scores_kernel,
        [
            ((parts, head, stack), F32),
            ((rows, head), F32),
            ((SPAN, rows, head), F32),
            ((SPAN, rows, head), BF16),
        ],
        [
            pltpu.VMEM((window, head), BF16),
            pltpu.VMEM((chunks, CHUNK, stack), F32),
            pltpu.VMEM((window, head), F32),
        ],
        20, 0,
        after(info, grad_value), query_stack, grad_stack, probs, key_window, value, *mine, *other,
    )
    got_k = core_swap(give_k)
    mine = [
        fan_out((mine_k[k] + got_k[k].astype(F32)).astype(BF16), k) for k in steps
    ]
    other = [core_swap(block) for block in mine]
    grad_input, grad_queries = call(
        finish_kernel,
        [((rows, depth), BF16), ((rows, heads * head), BF16)],
        [
            pltpu.VMEM((rows, depth), BF16),
            pltpu.VMEM((rows, heads * head), BF16),
            pltpu.SemaphoreType.DMA((9,)),
        ],
        12, 0,
        grad_value, full_weight, grad_stack_q,
    )
    grad_keys = sum_blocks(own_k, core_swap(own_k), mine, other).astype(BF16)
    return (grad_input, grad_queries, grad_keys, grad_weight)


def solution(mesh):
    in_specs = (
        P(("groups", "dp"), "fsdp"),
        P("fsdp", "dp"),
        P(("groups", "dp"), "fsdp"),
        P(("groups", "dp"), None),
        P(("groups", "dp"), "fsdp"),
        P("groups"),
        P("groups"),
    )
    out_specs = (
        P(("groups", "dp"), "fsdp"),
        P(("groups", "dp"), "fsdp"),
        P(("groups", "dp"), None),
        P(("groups", "fsdp"), "dp"),
    )
    return jax.shard_map(body, mesh=mesh, in_specs=in_specs, out_specs=out_specs, check_vma=False)
```

```python
import math

import jax
import jax.numpy as jnp
from jax import lax
from jax.experimental import pallas as pl
from jax.experimental.pallas import tpu as pltpu
from jax.sharding import PartitionSpec as P

SPAN = 3
NEGATIVE = -1e30
CHUNK = 256
ROWS = 128
BOTH = ("dp", "fsdp")
F32 = jnp.float32
BF16 = jnp.bfloat16
VMEM = pl.BlockSpec(memory_space=pltpu.VMEM)
SMEM = pl.BlockSpec(memory_space=pltpu.SMEM)
HBM = pl.BlockSpec(memory_space=pl.ANY)


def core_swap(value):
    return lax.ppermute(value, "fsdp", [(0, 1), (1, 0)])


def dp_swap(value, mask):
    count = lax.axis_size("dp")
    return lax.ppermute(value, "dp", [(i, i ^ mask) for i in range(count)])


def partner(step, me):
    turn = 1 - 2 * (me % 2)
    row = 2 - 4 * ((me // 2) % 2)
    return ((row, turn), (-3 * turn, -turn), (-row, 3 * turn))[step]


def offset(step, core):
    near, there = partner(step, lax.axis_index("dp"))
    return jnp.where(core == 0, near, there)


def fan_out(value, step):
    count = lax.axis_size("dp")
    pairs = [(2 * i + c, 2 * (i + partner(step, i)[c]) + c) for i in range(count) for c in (0, 1)]
    return lax.ppermute(value, BOTH, [(i, j) for i, j in pairs if 0 <= j < 2 * count])


def after(value, *others):
    return lax.optimization_barrier((value, *others))[0]


def chunk_range(first, window_first, docs_ref):
    last = first + ROWS - 1
    zero = jnp.int32(0)
    count = docs_ref.shape[0] // 2
    position = first + lax.broadcasted_iota(jnp.int32, (1, ROWS), 1)
    low, high = jnp.zeros((1, ROWS), jnp.int32), jnp.zeros((1, ROWS), jnp.int32)

    def step(doc, carry):
        start, least, most, low, high = carry
        length = docs_ref[doc]
        end = start + length
        bound = start + jnp.minimum(docs_ref[count + doc], length)
        least = jnp.where((start <= first) & (first < end), start, least)
        most = jnp.where((start <= last) & (last < end), jnp.maximum(last + 1, bound), most)
        inside = (position >= start) & (position < end)
        low = jnp.where(inside, start, low)
        high = jnp.where(inside, jnp.maximum(position + 1, bound), high)
        return (end, least, most, low, high)

    carry = (zero, zero, zero, low, high)
    if count <= 8:
        for doc in range(count):
            carry = step(doc, carry)
    else:
        carry = lax.fori_loop(0, count, step, carry)
    _, least, most, low, high = carry
    chunk_low = lax.div(least - window_first, CHUNK)
    chunk_high = lax.div(most - window_first + CHUNK - 1, CHUNK)
    return chunk_low, chunk_high, low, high


def at_block(index, rows):
    return pl.ds(pl.multiple_of(index * rows, rows), rows)


def place_window(core, window_ref, own, mine, other):
    rows = own.shape[0]
    window_ref[SPAN * rows : (SPAN + 1) * rows, :] = own
    for k in range(SPAN):
        window_ref[at_block(SPAN + offset(k, core), rows), :] = mine[k]
        window_ref[at_block(SPAN + offset(k, 1 - core), rows), :] = other[k]


def give_out(core, total_ref, own_ref, mine_ref, give_ref, factor):
    rows = own_ref.shape[0]
    own_ref[...] = total_ref[SPAN * rows : (SPAN + 1) * rows, :] * factor
    for k in range(SPAN):
        mine_ref[k] = total_ref[at_block(SPAN + offset(k, core), rows), :] * factor
        there = total_ref[at_block(SPAN + offset(k, 1 - core), rows), :] * factor
        give_ref[k] = there.astype(BF16)


def stack_heads(value, head):
    rows, wide = value.shape
    split = value.reshape(rows // ROWS, ROWS, wide // head, head)
    return split.transpose(0, 2, 1, 3).reshape(rows // ROWS, -1, head)


def nt_dot(a, b):
    return lax.dot_general(a, b, (((1,), (1,)), ((), ())), preferred_element_type=F32)


def tn_dot(a, b):
    return lax.dot_general(a, b, (((0,), (0,)), ((), ())), preferred_element_type=F32)


def fold(total, value, reduce):
    rows, lanes = value.shape
    return reduce(jnp.concatenate([total[None], value.reshape(rows // 8, 8, lanes)]), axis=0)


def limits_kernel(docs_ref, info_ref):
    rows = info_ref.shape[0] * ROWS
    first = lax.axis_index("dp") * rows
    window_first = first - SPAN * rows
    info_ref[...] = jnp.zeros_like(info_ref)
    for part in range(rows // ROWS):
        chunk_low, chunk_high, low, high = chunk_range(
            first + part * ROWS, window_first, docs_ref
        )
        info_ref[part, 0:1] = low - window_first
        info_ref[part, 1:2] = high - window_first
        info_ref[part, 2:3] = jnp.zeros_like(low) + chunk_low
        info_ref[part, 3:4] = jnp.zeros_like(low) + (chunk_high - chunk_low)


def by_count(count, most, body):
    for n in range(1, most + 1):

        @pl.when(count == n)
        def _():
            body(n)


def weights_kernel(
    info_ref, queries_ref, grads_ref, key_ref, r1, r2, r3, s1, s2, s3,
    probs_ref, window_ref, own_ref, mine_ref, give_ref,
    score_ref, total_ref,
):
    rows = key_ref.shape[0]
    stack = queries_ref.shape[1]
    core = lax.axis_index("fsdp")
    place_window(
        core, window_ref, key_ref[...], (r1[...], r2[...], r3[...]), (s1[...], s2[...], s3[...])
    )
    total_ref[...] = jnp.zeros_like(total_ref)
    power = math.log2(math.e) / math.sqrt(128.0)
    index = lax.broadcasted_iota(jnp.int32, (CHUNK, ROWS), 0)

    def part_step(part):
        chunk_low = info_ref[part, 2:3][0, 0]
        low = info_ref[part, 0:1] - chunk_low * CHUNK
        high = info_ref[part, 1:2] - chunk_low * CHUNK

        def chunks(count):
            peak = jnp.full((8, stack), NEGATIVE, F32)
            for i in range(count):
                scores = nt_dot(window_ref[at_block(chunk_low + i, CHUNK), :], queries_ref[part])
                place = index + i * CHUNK
                seen = (place >= low) & (place < high)
                seen = jnp.concatenate([seen] * (stack // ROWS), axis=1)
                masked = jnp.where(seen, scores, NEGATIVE)
                score_ref[i] = masked
                peak = fold(peak, masked, jnp.max)
            peak = jnp.max(peak, axis=0, keepdims=True)
            total = jnp.zeros((8, stack), F32)
            for i in range(count):
                probs = jnp.exp2((score_ref[i] - peak) * power)
                score_ref[i] = probs
                total = fold(total, probs, jnp.sum)
            inverse = 1.0 / jnp.sum(total, axis=0, keepdims=True)
            for i in range(count):
                probs = (score_ref[i] * inverse).astype(BF16)
                probs_ref[part, i] = probs
                total_ref[at_block(chunk_low + i, CHUNK), :] += jnp.dot(
                    probs, grads_ref[part], preferred_element_type=F32
                )

        by_count(info_ref[part, 3:4][0, 0], probs_ref.shape[1], chunks)

    for part in range(rows // ROWS):
        part_step(part)
    give_out(core, total_ref, own_ref, mine_ref, give_ref, 1.0)


def scores_kernel(
    info_ref, queries_ref, grads_ref, probs_ref, keys_ref, value_ref,
    r1, r2, r3, s1, s2, s3,
    query_ref, own_ref, mine_ref, give_ref,
    values_ref, product_ref, total_ref,
):
    rows = value_ref.shape[0]
    stack = queries_ref.shape[1]
    core = lax.axis_index("fsdp")
    place_window(core, values_ref, value_ref[...], (r1[0], r2[0], r3[0]), (s1[0], s2[0], s3[0]))
    total_ref[...] = jnp.zeros_like(total_ref)
    scaling = 1.0 / math.sqrt(128.0)

    def part_step(part, _):
        chunk_low = info_ref[part, 2:3][0, 0]

        def chunks(count):
            delta = jnp.zeros((8, stack), F32)
            for i in range(count):
                product = nt_dot(values_ref[at_block(chunk_low + i, CHUNK), :], grads_ref[part])
                product_ref[i] = product
                delta = fold(delta, product * probs_ref[part, i].astype(F32), jnp.sum)
            delta = jnp.sum(delta, axis=0, keepdims=True)
            query = jnp.zeros(query_ref.shape[1:], F32)
            for i in range(count):
                at = at_block(chunk_low + i, CHUNK)
                grad = (probs_ref[part, i].astype(F32) * (product_ref[i] - delta)).astype(BF16)
                total_ref[at, :] += jnp.dot(grad, queries_ref[part], preferred_element_type=F32)
                query += tn_dot(keys_ref[at, :], grad)
            query_ref[part] = query * scaling

        by_count(info_ref[part, 3:4][0, 0], probs_ref.shape[1], chunks)
        return 0

    lax.fori_loop(0, rows // ROWS, part_step, 0)
    give_out(core, total_ref, own_ref, mine_ref, give_ref, scaling)


def pack_kernel(half_ref, other_ref, mine_ref, got_ref, value_ref, *outs):
    value = (half_ref[...] + other_ref[...]).astype(BF16)
    value_ref[...] = value
    for k, out in enumerate(outs):
        out[0] = value
        out[1] = (mine_ref[k] + got_ref[k].astype(F32)).astype(BF16)


def sum_blocks(own, other, mine, others):
    total = own + other
    for a, b in zip(mine, others):
        total = total + (a.astype(F32) + b.astype(F32))
    return total


def value_kernel(x_ref, z0, z1, z2, z3, c0, c1, c2, c3, part_ref, weight_ref):
    me = lax.axis_index("dp")
    width = z0.shape[0]
    for k, (near, cross) in enumerate(((z0, c0), (z1, c1), (z2, c2), (z3, c3))):
        owner = me ^ (2 * k)
        weight_ref[pl.ds(pl.multiple_of(owner * width, width), width), :] = near[...]
        there = owner ^ 1
        weight_ref[pl.ds(pl.multiple_of(there * width, width), width), :] = cross[...]
    part_ref[...] = nt_dot(x_ref[...], weight_ref[...])


def weight_grad_kernel(x_ref, a_ref, b_ref, r1, r2, r3, s1, s2, s3, grad_ref, *outs):
    me = lax.axis_index("dp")
    grad = sum_blocks(
        a_ref[...], b_ref[...], (r1[1], r2[1], r3[1]), (s1[1], s2[1], s3[1])
    ).astype(BF16)
    grad_ref[...] = grad
    depth = x_ref.shape[1]
    width = outs[0].shape[0]
    step = 512
    scratch = outs[8]
    for at in range(0, depth, step):
        scratch[:, at : at + step] = tn_dot(grad, x_ref[:, at : at + step])
    for k in range(4):
        owner = me ^ (2 * k)
        outs[k][...] = scratch[pl.ds(pl.multiple_of(owner * width, width), width), :]
        there = owner ^ 1
        rows = scratch[pl.ds(pl.multiple_of(there * width, width), width), :]
        outs[4 + k][...] = rows.astype(BF16)


def finish_kernel(grad_ref, weight_ref, query_ref, out_hbm, query_hbm, out_ref, turned_ref, sems):
    copies = []
    for part in range(query_ref.shape[0]):
        for h in range(0, query_ref.shape[2], ROWS):
            turned_ref[part * ROWS : (part + 1) * ROWS, h : h + ROWS] = (
                query_ref[part, :, h : h + ROWS].T.astype(BF16)
            )
    copies.append(pltpu.make_async_copy(turned_ref, query_hbm, sems.at[8]))
    copies[-1].start()
    step = out_ref.shape[1] // 8
    for i in range(8):
        cut = slice(i * step, (i + 1) * step)
        out_ref[:, cut] = jnp.dot(
            grad_ref[...], weight_ref[:, cut], preferred_element_type=F32
        ).astype(BF16)
        copies.append(
            pltpu.make_async_copy(out_ref.at[:, cut], out_hbm.at[:, cut], sems.at[i])
        )
        copies[-1].start()
    for copy in copies:
        copy.wait()


def call(kernel, outs, scratch, limit_mib, smem, *args):
    return pl.pallas_call(
        kernel,
        in_specs=[SMEM] * smem + [VMEM] * (len(args) - smem),
        out_specs=[HBM if kernel is finish_kernel else VMEM for _ in outs],
        out_shape=[jax.ShapeDtypeStruct(shape, kind) for shape, kind in outs],
        scratch_shapes=scratch,
        compiler_params=pltpu.CompilerParams(vmem_limit_bytes=limit_mib << 20),
        cost_estimate=pl.CostEstimate(flops=1 << 30, bytes_accessed=4 << 20, transcendentals=0),
    )(*args)


def body(layer_input, w_value, queries, keys, grad_out, doc_lengths, prefix_spans):
    rows, depth = layer_input.shape
    head = keys.shape[1]
    heads = queries.shape[1] // head
    dp = lax.axis_size("dp")
    window = (2 * SPAN + 1) * rows
    chunks = window // CHUNK
    parts = rows // ROWS
    stack = heads * ROWS
    weight = w_value.T
    width = weight.shape[0]
    direct = dp == 8
    steps = range(SPAN)

    docs = jnp.concatenate([doc_lengths, prefix_spans])
    if direct:
        z3, z2, z1 = (dp_swap(weight, 2 * k) for k in (3, 2, 1))
        cross0 = dp_swap(weight, 1)
        docs = after(docs, cross0)
    (info,) = call(
        limits_kernel,
        [((parts, 8, ROWS), jnp.int32)],
        [], 4, 1,
        docs,
    )
    query_stack = stack_heads(queries, head)
    grad_stack = stack_heads(grad_out, head)
    mine = [fan_out(after(keys, info), k) for k in steps]
    other = [core_swap(after(block, z1, z2) if direct else block) for block in mine]

    if direct:
        cross = [cross0] + [dp_swap(block, 1) for block in (z1, z2, z3)]
        info = after(info, *cross[:3])

    probs, key_window, own_v, mine_v, give_v = call(
        weights_kernel,
        [
            ((parts, chunks, CHUNK, stack), BF16),
            ((window, head), BF16),
            ((rows, head), F32),
            ((SPAN, rows, head), F32),
            ((SPAN, rows, head), BF16),
        ],
        [
            pltpu.VMEM((chunks, CHUNK, stack), F32),
            pltpu.VMEM((window, head), F32),
        ],
        20, 0,
        info, query_stack, grad_stack, keys, *mine, *other,
    )
    got_v = core_swap(give_v)
    other_v = core_swap(own_v)

    if direct:
        value_part, full_weight = call(
            value_kernel,
            [((rows, head), F32), ((head, depth), BF16)],
            [], 12, 0,
            layer_input, weight, z1, z2, z3, *cross,
        )
    else:
        full_weight = lax.all_gather(weight, "dp", axis=0, tiled=True)
        value_part = nt_dot(layer_input, full_weight)
    value, *packs = call(
        pack_kernel,
        [((rows, head), BF16)] + [((2, rows, head), BF16)] * SPAN,
        [], 8, 0,
        value_part, core_swap(value_part), mine_v, got_v,
    )
    mine = [fan_out(pack, k) for pack, k in zip(packs, steps)]
    other = [core_swap(block) for block in mine]

    if direct:
        grad_value, *blocks = call(
            weight_grad_kernel,
            [((rows, head), BF16)] + [((width, depth), F32)] * 4 + [((width, depth), BF16)] * 4,
            [pltpu.VMEM((head, depth), F32)], 16, 0,
            layer_input, own_v, other_v, *mine, *other,
        )
        keep, send = blocks[:4], blocks[4:]
        total = keep[0]
        for k in (3, 2, 1):
            pair = (keep[k] + dp_swap(send[k], 1).astype(F32)).astype(BF16)
            total = total + dp_swap(pair, 2 * k).astype(F32)
        total = total + dp_swap(send[0], 1).astype(F32)
        grad_weight = total.T
    else:
        grad_value = sum_blocks(
            own_v, other_v, [block[1] for block in mine], [block[1] for block in other]
        ).astype(BF16)
        grad_weight = lax.psum_scatter(
            tn_dot(grad_value, layer_input), "dp", scatter_dimension=0, tiled=True
        ).T
    grad_stack_q, own_k, mine_k, give_k = call(
        scores_kernel,
        [
            ((parts, head, stack), F32),
            ((rows, head), F32),
            ((SPAN, rows, head), F32),
            ((SPAN, rows, head), BF16),
        ],
        [
            pltpu.VMEM((window, head), BF16),
            pltpu.VMEM((chunks, CHUNK, stack), F32),
            pltpu.VMEM((window, head), F32),
        ],
        20, 0,
        after(info, grad_value), query_stack, grad_stack, probs, key_window, value, *mine, *other,
    )
    got_k = core_swap(give_k)
    mine = [
        fan_out((mine_k[k] + got_k[k].astype(F32)).astype(BF16), k) for k in steps
    ]
    other = [core_swap(block) for block in mine]
    grad_input, grad_queries = call(
        finish_kernel,
        [((rows, depth), BF16), ((rows, heads * head), BF16)],
        [
            pltpu.VMEM((rows, depth), BF16),
            pltpu.VMEM((rows, heads * head), BF16),
            pltpu.SemaphoreType.DMA((9,)),
        ],
        12, 0,
        grad_value, full_weight, grad_stack_q,
    )
    grad_keys = sum_blocks(own_k, core_swap(own_k), mine, other).astype(BF16)
    return (grad_input, grad_queries, grad_keys, grad_weight)


def solution(mesh):
    in_specs = (
        P(("groups", "dp"), "fsdp"),
        P("fsdp", "dp"),
        P(("groups", "dp"), "fsdp"),
        P(("groups", "dp"), None),
        P(("groups", "dp"), "fsdp"),
        P("groups"),
        P("groups"),
    )
    out_specs = (
        P(("groups", "dp"), "fsdp"),
        P(("groups", "dp"), "fsdp"),
        P(("groups", "dp"), None),
        P(("groups", "fsdp"), "dp"),
    )
    return jax.shard_map(body, mesh=mesh, in_specs=in_specs, out_specs=out_specs, check_vma=False)
```
